128 devices in a mesh: gr: 8 (over x, core), gc: 16 (over z, y).
Axes of the slice: x: 4, y: 4, z: 4, core: 2. Of those that a mesh axis runs over, the one named last changes fastest.
Arguments:
- latent: float32 [8, 512, 16384], P(None, 'gr', 'gc'), may hold values from -12 to 12, as said below
- site_offset: float32 [8, 16384, 512], P(None, ('gr', 'gc')), may hold values from -6 to 6
- site_counts: int32 [8, 16384, 512], P(None, ('gr', 'gc')), may hold values from 0 to 4
- site_cells: int32 [16384, 512], P(('gr', 'gc')), may hold values from -1 to 65535, as said below
- detect_prob: float32 [8], replicated, may hold values from 0.15 to 0.6
- kappa_sq: float32 [8], replicated, may hold values from 0.002 to 0.04
Outputs:
- newton_step: float32 [8, 512, 16384], P(None, 'gr', 'gc')
- residual: float32 [8, 512, 16384], P(None, 'gr', 'gc')
The draws below stay inside these ranges and needn't reach their ends.
Inputs may be any that keep to these rules, and one draw needn't show every extreme that they name: `site_cells`: padding slots hold -1. In every row the live slots come first and there is at least one; the rows that a device sends to itself are full; the cells that a device receives vary widely in number from device to device. In every aligned block of 128 slots of a row, all live slots name cells of one and the same grid row of the owner's block. `latent`: latent values stay within the bounds.
All inputs are finite; a program needn't handle non-finite values.
Results may differ from the reference program's by a relative error of at most 0.0003.
Values sent between devices are 32-bit elements; how exact they have to be, the bound alone decides.
No kernel may reach another device: no remote copies, remote signals or barrier semaphores. Data moves between devices by JAX's collectives and lax.ppermute only.
A program may use at most 128 MiB of HBM per device.

```python
import math
import jax
import jax.numpy as jnp

K = 8
RD = 64
CD = 1024
SLOT = 512
SB = 128
VISITS = 4
ITERS = 2
NR = 512
NC = 16384
PAIRS = 16384
N_GR = 8
N_GC = 16


def shared_kappa(key):
    key_kappa = jax.random.fold_in(key, 7)
    low = math.log(0.002)
    high = math.log(0.04)
    values = jnp.exp(jax.random.uniform(key_kappa, (K,), jnp.float32, low, high))
    return jnp.clip(values, 0.002, 0.04)


def draw_kappa_sq(key, part):
    values = shared_kappa(key)
    return values.astype(jnp.float32)


def draw_site_cells(key, part):
    key = jax.random.fold_in(key, 11)
    devices = N_GR * N_GC
    blocks = SLOT // SB
    key_load, key_base, key_row, key_col = jax.random.split(key, 4)
    load = jax.random.randint(key_load, (devices, 1), 2, 6)
    base = jax.random.randint(key_base, (devices, devices), 0, SLOT)
    counts = jnp.clip(1 + base * load // 4, 1, SLOT)
    same = jnp.arange(devices)[:, None] == jnp.arange(devices)[None, :]
    counts = jnp.where(same, SLOT, counts).reshape(devices * devices, 1)
    block_row = jax.random.randint(key_row, (devices * devices, blocks), 0, RD)
    block_row = block_row.at[0, 0].set(RD - 1)
    slot_row = jnp.repeat(block_row, SB, axis=1)
    columns = jax.random.randint(key_col, (devices * devices, SLOT), 0, CD)
    columns = columns.at[0, 0].set(CD - 1)
    cells = slot_row * CD + columns
    slot_pos = jnp.arange(SLOT)[None, :]
    return jnp.where(slot_pos < counts, cells, -1).astype(jnp.int32)


def draw_latent(key, part):
    kappa = shared_kappa(key)
    key = jax.random.fold_in(key, 23)
    key_main = jax.random.fold_in(key, 0)
    amplitude = 0.25 / (4.0 * math.pi * 26.0 * kappa)
    column_scale = 3.0 ** (jnp.arange(NC, dtype=jnp.float32) / max(NC - 1, 1))
    row_wave = jnp.sin(math.pi * (jnp.arange(NR, dtype=jnp.float32) + 0.5) / NR)
    col_wave = jnp.sin(math.pi * (jnp.arange(NC, dtype=jnp.float32) + 0.5) / NC)
    bump = row_wave[:, None] * col_wave[None, :]
    rough = jnp.clip(jax.random.normal(key_main, (K, NR, NC), jnp.float32), -4.0, 4.0)
    smooth = 0.8 * bump
    values = rough * amplitude[:, None, None] * column_scale[None, None, :] + smooth[None, :, :]
    return jnp.clip(values, -12.0, 12.0).astype(jnp.float32)


def touch_ends(values, rng, low, high):
    longest = values.shape.index(max(values.shape))
    spots = []
    for shift in (0, 1):
        where = [jax.random.randint(jax.random.fold_in(rng, axis), (), 0, length) for axis, length in enumerate(values.shape)]
        where[longest] = (where[longest] + shift) % values.shape[longest]
        spots.append(tuple(where))
    return values.at[spots[0]].set(low).at[spots[1]].set(high)


def shard_levels(key, extent, pieces, least, high):
    factor_of = 1.0
    for axis_at, shards_of in pieces:
        steps = jax.random.uniform(jax.random.fold_in(jax.random.fold_in(key, 6), axis_at), (shards_of,), jnp.float32, least / len(pieces), high / len(pieces))
        factor_of = factor_of * jnp.repeat(jnp.exp(steps), extent[axis_at] // shards_of).reshape((-1,) + (1,) * (len(extent) - 1 - axis_at))
    return factor_of


def gaussian(rng, shape, width, bound, cuts=(), kind=jnp.bfloat16):
    loudness = shard_levels(rng, shape, cuts, -0.22, 0.18) if cuts else 1.0
    result = jax.random.normal(rng, shape, jnp.float32) * width * loudness
    return jnp.minimum(jnp.maximum(result, -bound), bound).astype(kind)


def setup_inputs(seed: int = 0) -> dict:
    keys = jax.random.split(jax.random.key(seed), 7)
    latent = draw_latent(jax.random.fold_in(keys[6], 71), 0)
    site_offset = gaussian(keys[1], (K, PAIRS, SLOT), 1.0, 6.0, ((1, 128),), jnp.float32)
    site_counts = touch_ends(jax.random.randint(keys[2], (K, PAIRS, SLOT), 0, VISITS + 1), jax.random.fold_in(keys[2], 1), 0, VISITS).astype(jnp.int32)
    site_cells = draw_site_cells(jax.random.fold_in(keys[6], 71), 0)
    detect_prob = jnp.clip(jax.random.uniform(keys[4], (K,), jnp.float32, 0.15, 0.6), 0.15, 0.6)
    kappa_sq = draw_kappa_sq(jax.random.fold_in(keys[6], 71), 0)
    return {"latent": latent, "site_offset": site_offset, "site_counts": site_counts, "site_cells": site_cells, "detect_prob": detect_prob, "kappa_sq": kappa_sq}


def factor_m(v, ksq):
    padded = jnp.pad(v, ((0, 0), (1, 1), (1, 1)))
    near = padded[:, 2:, 1:-1] + padded[:, :-2, 1:-1] + padded[:, 1:-1, 2:] + padded[:, 1:-1, :-2]
    return (ksq + 4.0) * v - near


def prior_apply(v, ksq):
    return (4.0 * math.pi * ksq) * factor_m(factor_m(v, ksq), ksq)


def reference(latent, site_offset, site_counts, site_cells, detect_prob, kappa_sq):
    devices = N_GR * N_GC
    ksq = kappa_sq[:, None, None]
    q_inverse = (1.0 - detect_prob) ** (-VISITS)
    ratio = jnp.where(site_counts > 0, jnp.zeros_like(site_offset), q_inverse[:, None, None] * jnp.ones_like(site_offset))
    ratio = ratio.reshape(K, devices, devices, SLOT).transpose(0, 2, 1, 3).reshape(K, -1)
    offsets = site_offset.reshape(K, devices, devices, SLOT).transpose(0, 2, 1, 3).reshape(K, -1)
    owner = jnp.arange(devices * devices, dtype=jnp.int32) // devices
    valid = site_cells >= 0
    safe = jnp.where(valid, site_cells, 0)
    grid_row = (owner // N_GC)[:, None] * RD + safe // CD
    grid_col = (owner % N_GC)[:, None] * CD + safe % CD
    flat_index = (grid_row * NC + grid_col).reshape(-1).astype(jnp.int32)
    live = valid.reshape(-1).astype(latent.dtype)
    latent_flat = latent.reshape(K, NR * NC)
    eta = latent_flat[:, flat_index] + offsets
    psi = jax.nn.sigmoid(eta)
    spread = psi * (1.0 - psi)
    weight = spread * live
    gradient = spread * (1.0 - ratio) / (psi + (1.0 - psi) * ratio) * live
    cell_weight = jnp.zeros_like(latent_flat).at[:, flat_index].add(weight).reshape(K, NR, NC)
    cell_grad = jnp.zeros_like(latent_flat).at[:, flat_index].add(gradient).reshape(K, NR, NC)
    right_side = cell_grad - prior_apply(latent, ksq)
    newton_step = jnp.zeros_like(latent)
    residual = right_side
    direction = right_side
    norm_now = jnp.sum(residual * residual)
    for step in range(ITERS):
        image = prior_apply(direction, ksq) + cell_weight * direction
        alpha = norm_now / jnp.sum(direction * image)
        newton_step = newton_step + alpha * direction
        residual = residual - alpha * image
        norm_next = jnp.sum(residual * residual)
        direction = residual + (norm_next / norm_now) * direction
        norm_now = norm_next
    return newton_step, residual
```

```python
import functools
import math

import jax
import jax.numpy as jnp
from jax import lax
from jax.experimental import pallas as pl
from jax.experimental.pallas import tpu as pltpu
from jax.sharding import PartitionSpec as P

SB = 128
VISITS = 4
LANES = 128
MESH = ("gr", "gc")
VMEM = pltpu.VMEM
SMEM = pltpu.SMEM
F32 = jnp.float32
BF16 = jnp.bfloat16


def whole(space=VMEM):
    return pl.BlockSpec(memory_space=space)


def params(mib):
    return pltpu.CompilerParams(vmem_limit_bytes=mib * 1024 * 1024)


def cost(flops, moved):
    return pl.CostEstimate(flops=flops, bytes_accessed=moved, transcendentals=0)


def pack_kernel(q_ref, offset_ref, counts_ref, out_ref):
    species = offset_ref.shape[0]
    offsets = jnp.swapaxes(offset_ref[...], 0, 1)
    counts = jnp.swapaxes(counts_ref[...], 0, 1)
    q = q_ref[...][None, :, :1]
    out_ref[:, :species, :] = offsets
    out_ref[:, species:, :] = jnp.where(counts > 0, jnp.zeros_like(offsets), q)


def pack_sites(site_offset, site_counts, q_inverse):
    species, owners, slots = site_offset.shape
    group = 8
    block = pl.BlockSpec((species, group, slots), lambda i: (0, i, 0))
    return pl.pallas_call(
        pack_kernel,
        grid=(owners // group,),
        in_specs=[pl.BlockSpec((species, LANES), lambda i: (0, 0)), block, block],
        out_specs=pl.BlockSpec((group, 2 * species, slots), lambda i: (i, 0, 0)),
        out_shape=jax.ShapeDtypeStruct((owners, 2 * species, slots), F32),
        compiler_params=params(32),
        name="pack_sites",
    )(jnp.broadcast_to(q_inverse[:, None], (species, LANES)), site_offset, site_counts)


def factor_row(field_ref, row, ksq4):
    width = field_ref.shape[2]
    center = field_ref[row]
    near = field_ref[row - 1] + field_ref[row + 1]
    near = near + pltpu.roll(center, 1, 1) + pltpu.roll(center, width - 1, 1)
    return ksq4 * center - near


def column_mask(edge_ref, width):
    lane = lax.broadcasted_iota(jnp.int32, (1, width), 1)
    right = edge_ref[3].astype(F32)
    left = edge_ref[2].astype(F32)
    own = width - LANES
    return jnp.where(lane < own, 1.0, jnp.where(lane < own + LANES // 2, right, left))


def factor_pass(src_ref, dst_ref, first, last, halo_low, halo_high, edge_ref, ksq4, unroll=2):
    cols = column_mask(edge_ref, src_ref.shape[2])
    up = edge_ref[0].astype(F32)
    down = edge_ref[1].astype(F32)

    def step(row, carry):
        scale = jnp.where(row < halo_low, up, jnp.where(row >= halo_high, down, 1.0))
        dst_ref[row] = factor_row(src_ref, row, ksq4) * (cols * scale)
        return carry

    lax.fori_loop(first, last, step, 0, unroll=unroll)


def latent_prior_kernel(edge_ref, ksq_ref, lat_ref, out_ref, mid_ref):
    rows = out_ref.shape[0]
    own = out_ref.shape[2]
    ksq = ksq_ref[:, :1]
    ksq4 = ksq + 4.0
    factor_pass(lat_ref, mid_ref, 1, rows + 3, 2, rows + 2, edge_ref, ksq4)
    scale = -4.0 * math.pi * ksq

    def step(row, carry):
        out_ref[row] = scale * factor_row(mid_ref, row + 2, ksq4)[:, :own]
        return carry

    lax.fori_loop(0, rows, step, 0, unroll=2)


def latent_prior(edges, ksq, lat_ext, rows, cols):
    species = lat_ext.shape[1]
    return pl.pallas_call(
        latent_prior_kernel,
        in_specs=[whole(SMEM), whole(), whole()],
        out_specs=whole(),
        out_shape=jax.ShapeDtypeStruct((rows, species, cols), F32),
        scratch_shapes=[VMEM(lat_ext.shape, F32)],
        compiler_params=params(24),
        cost_estimate=cost(20 * rows * species * cols, 16 * rows * species * cols),
        name="latent_prior",
    )(edges, ksq, lat_ext)


def gather_kernel(rows_ref, cells_ref, lat_ref, out_ref):
    group, blocks = cells_ref.shape[:2]
    species = lat_ref.shape[1]
    tiles = lat_ref.shape[2] // LANES
    base = pl.program_id(0) * group

    def step(source, carry):
        for j in range(blocks):
            row = rows_ref[(base + source) * blocks + j]
            cell = cells_ref[source, j:j + 1, :]
            cell = jnp.broadcast_to(cell, (species, SB))
            low = cell & (LANES - 1)
            high = (cell // LANES) & (tiles - 1)
            value = jnp.zeros((species, SB), F32)
            for t in range(tiles):
                part = lat_ref[row, :, t * LANES:(t + 1) * LANES]
                picked = jnp.take_along_axis(part, low, axis=1)
                value = jnp.where(high == t, picked, value)
            out_ref[source, :, j * SB:(j + 1) * SB] = value
        return carry

    lax.fori_loop(0, group, step, 0)


def gather_latent(block_rows, site_cells, lat_rows):
    sources, blocks, lanes = site_cells.shape
    slots = blocks * lanes
    rows, species, cols = lat_rows.shape
    group = 16
    return pl.pallas_call(
        gather_kernel,
        grid=(sources // group,),
        in_specs=[
            whole(SMEM),
            pl.BlockSpec((group, blocks, lanes), lambda i: (i, 0, 0)),
            pl.BlockSpec((rows, species, cols), lambda i: (0, 0, 0)),
        ],
        out_specs=pl.BlockSpec((group, species, slots), lambda i: (i, 0, 0)),
        out_shape=jax.ShapeDtypeStruct((sources, species, slots), F32),
        compiler_params=params(24),
        cost_estimate=cost(16 * sources * slots * species, 8 * sources * slots * species),
        name="gather_latent",
    )(block_rows, site_cells, lat_rows)


def hi_lo(value):
    high = value.astype(BF16)
    low = (value - high.astype(F32)).astype(BF16)
    return high, low


def strip_pack(field_ref, width, side):
    rows = field_ref.shape[0]
    cols = field_ref.shape[2]
    species = field_ref.shape[1]
    per_tile = LANES // width
    lane = lax.broadcasted_iota(jnp.int32, (species, LANES), 1) // width
    tiles = []
    for tile in range(rows // per_tile):
        packed = jnp.zeros((species, LANES), F32)
        for p in range(per_tile):
            row = tile * per_tile + p
            if side == 0:
                part = field_ref[row, :, :LANES]
                shift = (p * width) % LANES
            else:
                part = field_ref[row, :, cols - LANES:]
                shift = (p * width + width) % LANES
            if shift:
                part = pltpu.roll(part, shift, 1)
            packed = jnp.where(lane == p, part, packed)
        tiles.append(packed)
    return tiles


def site_kernel(rows_ref, cells_ref, sites_ref, values_ref, prior_ref,
                b_ref, w_ref, left_ref, right_ref, up_ref, down_ref):
    group, blocks = cells_ref.shape[:2]
    species = values_ref.shape[1]
    rows = b_ref.shape[0]
    cols = b_ref.shape[2]
    tiles = cols // LANES
    step_id = pl.program_id(0)
    base = step_id * group

    @pl.when(step_id == 0)
    def _():
        b_ref[...] = prior_ref[...]
        w_ref[...] = jnp.zeros_like(w_ref)

    lane_of = lax.broadcasted_iota(jnp.int32, (LANES, SB), 0).astype(jnp.int16)
    one = jnp.ones((LANES, SB), BF16)
    zero = jnp.zeros((LANES, SB), BF16)
    zero16 = jnp.zeros((2 * species, SB), BF16)

    def step(source, carry):
        for j in range(blocks):
            row = rows_ref[(base + source) * blocks + j]
            spot = pl.ds(j * SB, SB)
            cell = cells_ref[source, j:j + 1, :]
            low = (cell & (LANES - 1)).astype(jnp.int16)
            high = jnp.where(cell < 0, -1, (cell // LANES) & (tiles - 1)).astype(jnp.int16)
            high = jnp.broadcast_to(high, (2 * species, SB))
            eta = values_ref[source, :, spot] + sites_ref[source, :species, spot]
            ratio = sites_ref[source, species:, spot]
            e = jnp.exp(-eta)
            psi = 1.0 / (1.0 + e)
            ep = e * psi
            weight = ep * psi
            gradient = ep * (1.0 - ratio) / (1.0 + e * ratio)
            both_hi, both_lo = hi_lo(jnp.concatenate([weight, gradient], axis=0))
            hot = jnp.where(lane_of == jnp.broadcast_to(low, (LANES, SB)), one, zero)
            placed_hi = []
            placed_lo = []
            for t in range(tiles):
                here = high == t
                placed_hi.append(jnp.where(here, both_hi, zero16))
                placed_lo.append(jnp.where(here, both_lo, zero16))
            left = jnp.concatenate(
                [jnp.concatenate(placed_hi, axis=0), jnp.concatenate(placed_lo, axis=0)], axis=1
            )
            right = jnp.concatenate([hot, hot], axis=1)
            placed = lax.dot_general(
                left, right, (((1,), (1,)), ((), ())), preferred_element_type=F32
            )
            for t in range(tiles):
                at = 2 * species * t
                lanes = pl.ds(t * LANES, LANES)
                w_ref[row, :, lanes] += placed[at:at + species]
                b_ref[row, :, lanes] += placed[at + species:at + 2 * species]
        return carry

    lax.fori_loop(0, group, step, 0)

    @pl.when(step_id == pl.num_programs(0) - 1)
    def _():
        for side, ref in ((0, left_ref), (1, right_ref)):
            strips = strip_pack(b_ref, 4, side) + strip_pack(w_ref, 2, side)
            for i, strip in enumerate(strips):
                ref[i] = strip
        for ref, b0, w0 in ((up_ref, 0, 0), (down_ref, rows - 4, rows - 2)):
            for i in range(6):
                for t in range(tiles):
                    lanes = pl.ds(t * LANES, LANES)
                    if i < 4:
                        ref[i * tiles + t] = b_ref[b0 + i, :, lanes]
                    else:
                        ref[i * tiles + t] = w_ref[w0 + i - 4, :, lanes]
            for i in range(6 * tiles, ref.shape[0]):
                ref[i] = jnp.zeros((species, LANES), F32)


def site_terms(block_rows, site_cells, sites, values, prior):
    sources, blocks, lanes = site_cells.shape
    slots = blocks * lanes
    rows, species, cols = prior.shape
    group = 16
    strip_tiles = 6 * rows // LANES
    edge_tiles = 6 * (cols // LANES) + 2 * strip_tiles
    const = lambda i: (0, 0, 0)
    field = pl.BlockSpec((rows, species, cols), const)
    strip = pl.BlockSpec((strip_tiles, species, LANES), const)
    edge = pl.BlockSpec((edge_tiles, species, LANES), const)
    shape = lambda *s: jax.ShapeDtypeStruct(s, F32)
    return pl.pallas_call(
        site_kernel,
        grid=(sources // group,),
        in_specs=[
            whole(SMEM),
            pl.BlockSpec((group, blocks, lanes), lambda i: (i, 0, 0)),
            pl.BlockSpec((group, 2 * species, slots), lambda i: (i, 0, 0)),
            pl.BlockSpec((group, species, slots), lambda i: (i, 0, 0)),
            field,
        ],
        out_specs=[field, field, strip, strip, edge, edge],
        out_shape=[
            shape(rows, species, cols),
            shape(rows, species, cols),
            shape(strip_tiles, species, LANES),
            shape(strip_tiles, species, LANES),
            shape(edge_tiles, species, LANES),
            shape(edge_tiles, species, LANES),
        ],
        compiler_params=params(40),
        name="site_terms",
    )(block_rows, site_cells, sites, values, prior)


def halo_tile(right_tiles, left_tiles, row, width, lane):
    per_tile = LANES // width
    tile, p = row // per_tile, row % per_tile
    from_right = pltpu.roll(right_tiles[tile], (LANES - p * width) % LANES, 1) if p else right_tiles[tile]
    shift = (LANES - p * width - width) % LANES
    from_left = pltpu.roll(left_tiles[tile], shift, 1) if shift else left_tiles[tile]
    return jnp.where(lane < width, from_right, jnp.where(lane >= LANES - width, from_left, 0.0))


def krylov_kernel(edge_ref, ksq_ref, b_ref, w_ref, right_ref, left_ref, up_ref, down_ref,
                  h_out, h2_out, part_ref, bx, wx, m_ref, hx):
    rows, species, cols = b_ref.shape
    tiles = cols // LANES
    ksq = ksq_ref[:, :1]
    ksq4 = ksq + 4.0
    scale = 4.0 * math.pi * ksq
    own = pl.ds(0, cols)
    halo = pl.ds(cols, LANES)
    lane = lax.broadcasted_iota(jnp.int32, (species, LANES), 1)
    bx[4:rows + 4, :, own] = b_ref[...]
    wx[2:rows + 2, :, own] = w_ref[...]
    b_tiles = 4 * rows // LANES
    strip_tiles = 6 * rows // LANES

    def strips(ref, base):
        both = [ref[base + i] for i in range(strip_tiles)]
        return both[:b_tiles], both[b_tiles:]

    rb, rw = strips(right_ref, 0)
    lb, lw = strips(left_ref, 0)
    for row in range(rows):
        bx[4 + row, :, halo] = halo_tile(rb, lb, row, 4, lane)
        wx[2 + row, :, halo] = halo_tile(rw, lw, row, 2, lane)
    edge = 6 * tiles
    for ref, b_to, w_to, b_from, w_from in (
        (up_ref, 0, 0, rows - 4, rows - 2),
        (down_ref, rows + 4, rows + 2, 0, 0),
    ):
        rb, rw = strips(ref, edge)
        lb, lw = strips(ref, edge + strip_tiles)
        for i in range(4):
            for t in range(tiles):
                bx[b_to + i, :, pl.ds(t * LANES, LANES)] = ref[i * tiles + t]
            bx[b_to + i, :, halo] = halo_tile(rb, lb, b_from + i, 4, lane)
        for i in range(2):
            for t in range(tiles):
                wx[w_to + i, :, pl.ds(t * LANES, LANES)] = ref[(4 + i) * tiles + t]
            wx[w_to + i, :, halo] = halo_tile(rw, lw, w_from + i, 2, lane)

    factor_pass(bx, m_ref, 1, rows + 7, 4, rows + 4, edge_ref, ksq4)
    columns = column_mask(edge_ref, bx.shape[2])
    up = edge_ref[0].astype(F32)
    down = edge_ref[1].astype(F32)

    def first(row, carry):
        mask = columns * jnp.where(row < 4, up, jnp.where(row >= rows + 4, down, 1.0))
        hx[row] = (scale * factor_row(m_ref, row, ksq4) + wx[row - 2] * bx[row]) * mask
        return carry

    lax.fori_loop(2, rows + 6, first, 0, unroll=2)
    factor_pass(hx, m_ref, 3, rows + 5, 4, rows + 4, edge_ref, ksq4)

    zero = jnp.zeros((species, cols), F32)

    def second(row, sums):
        bb, bh, hh, hh2 = sums
        b = bx[row + 4, :, own]
        h = hx[row + 4, :, own]
        h2 = scale * factor_row(m_ref, row + 4, ksq4)[:, :cols] + wx[row + 2, :, own] * h
        h_out[row] = h
        h2_out[row] = h2
        return (bb + b * b, bh + b * h, hh + h * h, hh2 + h * h2)

    sums = lax.fori_loop(0, rows, second, (zero, zero, zero, zero))
    lane_row = lax.broadcasted_iota(jnp.int32, part_ref.shape, 1)
    part = jnp.zeros(part_ref.shape, F32)
    for i, total in enumerate(sums):
        narrow = total[:, :LANES]
        for t in range(1, tiles):
            narrow = narrow + total[:, t * LANES:(t + 1) * LANES]
        narrow = jnp.sum(narrow, axis=0, keepdims=True)
        narrow = jnp.sum(narrow, axis=1, keepdims=True)
        part = jnp.where(lane_row == i, narrow, part)
    part_ref[...] = part


def krylov(edges, ksq, b, w, right, left, from_up, from_down, devices):
    rows, species, cols = b.shape
    ext = VMEM((rows + 8, species, cols + LANES), F32)
    shape = lambda *s: jax.ShapeDtypeStruct(s, F32)
    return pl.pallas_call(
        krylov_kernel,
        in_specs=[whole(SMEM)] + [whole()] * 7,
        out_specs=[whole()] * 3,
        out_shape=[shape(rows, species, cols), shape(rows, species, cols), shape(devices, LANES)],
        scratch_shapes=[ext, VMEM((rows + 4, species, cols + LANES), F32), ext, ext],
        compiler_params=params(40),
        name="krylov",
    )(edges, ksq, b, w, right, left, from_up, from_down)


def finish_kernel(parts_ref, b_ref, h_ref, h2_ref, step_ref, residual_ref):
    total = jnp.sum(parts_ref[...], axis=0, keepdims=True)
    lane = lax.broadcasted_iota(jnp.int32, total.shape, 1)

    def pick(i):
        return jnp.sum(jnp.where(lane == i, total, 0.0), axis=1, keepdims=True)

    bb, bh, hh, hh2 = (pick(i) for i in range(4))
    alpha = bb / bh
    rr = bb - 2.0 * alpha * bh + alpha * alpha * hh
    beta = rr / bb
    grown = 1.0 + beta
    curve = grown * grown * bh - 2.0 * grown * alpha * hh + alpha * alpha * hh2
    later = rr / curve
    c0 = alpha + later * grown
    c1 = later * alpha
    b = b_ref[...]
    h = h_ref[...]
    c0 = c0[None]
    c1 = c1[None]
    step_ref[...] = jnp.swapaxes(c0 * b - c1 * h, 0, 1)
    residual_ref[...] = jnp.swapaxes(b - c0 * h + c1 * h2_ref[...], 0, 1)


def finish(parts, b, h, h2):
    rows, species, cols = b.shape
    group = 8
    field = pl.BlockSpec((group, species, cols), lambda i: (i, 0, 0))
    out = pl.BlockSpec((species, group, cols), lambda i: (0, i, 0))
    shape = jax.ShapeDtypeStruct((species, rows, cols), F32)
    return pl.pallas_call(
        finish_kernel,
        grid=(rows // group,),
        in_specs=[pl.BlockSpec(parts.shape, lambda i: (0, 0)), field, field, field],
        out_specs=[out, out],
        out_shape=[shape, shape],
        compiler_params=params(24),
        name="finish",
    )(parts, b, h, h2)


def neighbour_pairs(count):
    forward = [(i, i + 1) for i in range(count - 1)]
    backward = [(target, source) for source, target in forward]
    return forward, backward


def per_device(latent, site_offset, site_counts, site_cells, detect_prob, kappa_sq):
    species, rows, cols = latent.shape
    n_gr, n_gc = lax.axis_size("gr"), lax.axis_size("gc")
    gr, gc = lax.axis_index("gr"), lax.axis_index("gc")
    down_pairs, up_pairs = neighbour_pairs(n_gr)
    right_pairs, left_pairs = neighbour_pairs(n_gc)
    q_inverse = (1.0 - detect_prob) ** (-VISITS)
    sites = lax.all_to_all(
        pack_sites(site_offset, site_counts, q_inverse), MESH, split_axis=0, concat_axis=0, tiled=True
    )
    edges = jnp.stack([gr > 0, gr < n_gr - 1, gc > 0, gc < n_gc - 1]).astype(jnp.int32)
    ksq = jnp.broadcast_to(kappa_sq[:, None], (species, LANES))
    site_cells = site_cells.reshape(site_cells.shape[0], -1, SB)
    block_rows = (jnp.maximum(site_cells[:, :, 0], 0) // cols).reshape(-1)

    lat_rows = jnp.transpose(latent, (1, 0, 2))
    above = lax.ppermute(lat_rows[-2:], "gr", down_pairs)
    below = lax.ppermute(lat_rows[:2], "gr", up_pairs)
    lat_ext = jnp.concatenate([above, lat_rows, below], axis=0)
    left = lax.ppermute(lat_ext[:, :, -2:], "gc", right_pairs)
    right = lax.ppermute(lat_ext[:, :, :2], "gc", left_pairs)
    gap = jnp.zeros((rows + 4, species, LANES - 4), F32)
    lat_ext = jnp.concatenate([lat_ext, right, gap, left], axis=2)
    prior = latent_prior(edges, ksq, lat_ext, rows, cols)
    values = gather_latent(block_rows, site_cells, lat_rows)

    b, w, to_left, to_right, to_up, to_down = site_terms(block_rows, site_cells, sites, values, prior)
    from_left = lax.ppermute(to_right, "gc", right_pairs)
    from_right = lax.ppermute(to_left, "gc", left_pairs)
    strips = jnp.concatenate([from_right, from_left], axis=0)
    spot = (to_up.shape[0] - strips.shape[0], 0, 0)
    to_up = lax.dynamic_update_slice(to_up, strips, spot)
    to_down = lax.dynamic_update_slice(to_down, strips, spot)
    from_up = lax.ppermute(to_down, "gr", down_pairs)
    from_down = lax.ppermute(to_up, "gr", up_pairs)

    h, h2, part = krylov(edges, ksq, b, w, from_right, from_left, from_up, from_down, n_gr * n_gc)
    parts = lax.all_to_all(part, MESH, split_axis=0, concat_axis=0, tiled=True)
    return finish(parts, b, h, h2)


def solution(mesh):
    in_specs = (
        P(None, "gr", "gc"),
        P(None, ("gr", "gc"), None),
        P(None, ("gr", "gc"), None),
        P(("gr", "gc"), None),
        P(),
        P(),
    )
    out_specs = (P(None, "gr", "gc"), P(None, "gr", "gc"))
    return jax.shard_map(
        per_device, mesh=mesh, in_specs=in_specs, out_specs=out_specs, check_vma=False
    )
```

```python
import functools
import math

import jax
import jax.numpy as jnp
from jax import lax
from jax.experimental import pallas as pl
from jax.experimental.pallas import tpu as pltpu
from jax.sharding import PartitionSpec as P

SB = 128
VISITS = 4
LANES = 128
MESH = ("gr", "gc")
VMEM = pltpu.VMEM
SMEM = pltpu.SMEM
F32 = jnp.float32
BF16 = jnp.bfloat16


def whole(space=VMEM):
    return pl.BlockSpec(memory_space=space)


def params(mib):
    return pltpu.CompilerParams(vmem_limit_bytes=mib * 1024 * 1024)


def anywhere():
    return pl.BlockSpec(memory_space=pl.ANY)


def dma(count):
    return pltpu.SemaphoreType.DMA((count,))


def cost(flops, moved):
    return pl.CostEstimate(flops=flops, bytes_accessed=moved, transcendentals=0)


def pack_kernel(prob_ref, offset_hbm, counts_hbm, out_hbm, offset, counts, out, in_sem, out_sem):
    species, owners, slots = offset.shape
    pieces = in_sem.shape[0] // 2
    size = owners // pieces
    loads = []
    for p in range(pieces):
        part = pl.ds(p * size, size)
        for i, (src, dst) in enumerate(((offset_hbm, offset), (counts_hbm, counts))):
            copy = pltpu.make_async_copy(src.at[:, part], dst.at[:, part], in_sem.at[2 * p + i])
            copy.start()
            loads.append(copy)
    row = lax.broadcasted_iota(jnp.int32, (species, LANES), 0)
    prob = jnp.zeros((species, LANES), F32)
    for k in range(species):
        prob = jnp.where(row == k, prob_ref[k], prob)
    square = (1.0 - prob) * (1.0 - prob)
    q = (1.0 / (square * square))[None]
    group = 8
    stores = []
    for p in range(pieces):
        loads[2 * p].wait()
        loads[2 * p + 1].wait()

        def turn(i, carry):
            rows = pl.ds(pl.multiple_of(p * size + i * group, group), group)
            for t in range(slots // LANES):
                lanes = pl.ds(t * LANES, LANES)
                offsets = jnp.swapaxes(offset[:, rows, lanes], 0, 1)
                found = jnp.swapaxes(counts[:, rows, lanes], 0, 1)
                out[rows, :species, lanes] = offsets
                out[rows, species:, lanes] = jnp.where(found > 0, jnp.zeros_like(offsets), q)
            return carry

        lax.fori_loop(0, size // group, turn, 0)
        part = pl.ds(p * size, size)
        copy = pltpu.make_async_copy(out.at[part], out_hbm.at[part], out_sem.at[p])
        copy.start()
        stores.append(copy)
    for copy in stores:
        copy.wait()


def pack_sites(site_offset, site_counts, detect_prob):
    species, owners, slots = site_offset.shape
    pieces = 4
    return pl.pallas_call(
        pack_kernel,
        in_specs=[whole(SMEM), anywhere(), anywhere()],
        out_specs=anywhere(),
        out_shape=jax.ShapeDtypeStruct((owners, 2 * species, slots), F32),
        scratch_shapes=[
            VMEM(site_offset.shape, F32),
            VMEM(site_offset.shape, jnp.int32),
            VMEM((owners, 2 * species, slots), F32),
            dma(2 * pieces),
            dma(pieces),
        ],
        compiler_params=params(56),
        name="pack_sites",
    )(detect_prob, site_offset, site_counts)


def load_row(ref, row):
    return [ref[row, :, t * LANES:(t + 1) * LANES] for t in range(ref.shape[2] // LANES)]


def store_row(ref, row, tiles):
    for t, tile in enumerate(tiles):
        ref[row, :, t * LANES:(t + 1) * LANES] = tile


def factor_row(ref, row, ksq4, lane, count=None):
    center = load_row(ref, row)
    above = load_row(ref, row - 1)
    below = load_row(ref, row + 1)
    total = len(center)
    right = [pltpu.roll(tile, 1, 1) for tile in center]
    left = [pltpu.roll(tile, LANES - 1, 1) for tile in center]
    out = []
    for t in range(count or total):
        from_left = jnp.where(lane == 0, right[t - 1], right[t])
        from_right = jnp.where(lane == LANES - 1, left[(t + 1) % total], left[t])
        out.append(ksq4 * center[t] - ((above[t] + below[t]) + (from_left + from_right)))
    return out


def each_row(first, last, body, chunk=16):
    turns = (last - first) // chunk

    def turn(i, carry):
        for u in range(chunk):
            body(first + i * chunk + u)
        return carry

    lax.fori_loop(0, turns, turn, 0)
    for row in range(first + turns * chunk, last):
        body(row)


class Edges:
    def __init__(self, edge_ref, lane):
        self.up, self.down, left, right = (edge_ref[i].astype(F32) for i in range(4))
        self.halo = jnp.where(lane < LANES // 2, right, left)

    def pass_rows(self, first, last, low, high, row_tiles, dst_ref):
        def put(row, scale):
            tiles = row_tiles(row)
            tiles[-1] = tiles[-1] * self.halo
            if scale is not None:
                tiles = [tile * scale for tile in tiles]
            store_row(dst_ref, row, tiles)

        for row in range(first, low):
            put(row, self.up)
        each_row(low, high, lambda row: put(row, None))
        for row in range(high, last):
            put(row, self.down)


def strip_pack(field_ref, width, side):
    rows, species, cols = field_ref.shape
    per_tile = LANES // width
    lane = lax.broadcasted_iota(jnp.int32, (species, LANES), 1) // width
    tiles = []
    for tile in range(rows // per_tile):
        packed = jnp.zeros((species, LANES), F32)
        for p in range(per_tile):
            row = tile * per_tile + p
            if side == 0:
                part = field_ref[row, :, :LANES]
                shift = (p * width) % LANES
            else:
                part = field_ref[row, :, cols - LANES:]
                shift = (p * width + width) % LANES
            if shift:
                part = pltpu.roll(part, shift, 1)
            packed = jnp.where(lane == p, part, packed)
        tiles.append(packed)
    return tiles


def halo_tile(right_tiles, left_tiles, row, width, lane):
    per_tile = LANES // width
    tile, p = row // per_tile, row % per_tile
    shift = (LANES - p * width) % LANES
    from_right = pltpu.roll(right_tiles[tile], shift, 1) if shift else right_tiles[tile]
    shift = (LANES - p * width - width) % LANES
    from_left = pltpu.roll(left_tiles[tile], shift, 1) if shift else left_tiles[tile]
    return jnp.where(lane < width, from_right, jnp.where(lane >= LANES - width, from_left, 0.0))


WIDTHS = (8, 4, 2)
DEPTHS = (6, 4, 2)
TURN = 32
STAGES = 4


def strip_counts(rows):
    return [rows * width // LANES for width in WIDTHS]


def gather_kernel(first_ref, cells_ref, lat_ref, values_ref, cells_out, list_ref, row_ref, count_ref,
                  left_ref, right_ref):
    sources, blocks = cells_ref.shape[:2]
    species, cols = lat_ref.shape[1:]
    tiles = cols // LANES
    total = sources * blocks
    per_stage = sources // STAGES

    def step(source, spot):
        for j in range(blocks):
            cell = cells_ref[source, j:j + 1, :]
            first = first_ref[source * blocks + j]
            row = jnp.maximum(first, 0) // cols
            live = first >= 0
            at = jnp.where(live, spot, total + TURN)
            wide = jnp.broadcast_to(cell, (species, SB))
            low = wide & (LANES - 1)
            high = (wide // LANES) & (tiles - 1)
            value = jnp.zeros((species, SB), F32)
            for t in range(tiles):
                part = lat_ref[row, :, t * LANES:(t + 1) * LANES]
                picked = jnp.take_along_axis(part, low, axis=1)
                value = jnp.where(high == t, picked, value)
            values_ref[at] = value
            cells_out[at] = cell
            list_ref[at] = source * blocks + j
            row_ref[at] = row
            spot = spot + live.astype(jnp.int32)
        return spot

    count = jnp.int32(0)
    for stage in range(STAGES):
        count_ref[stage] = count
        count = lax.fori_loop(stage * per_stage, (stage + 1) * per_stage, step, count)
    count_ref[STAGES] = count
    for u in range(TURN):
        values_ref[count + u] = jnp.zeros((species, SB), F32)
        cells_out[count + u] = jnp.full((1, SB), -1, jnp.int32)
        list_ref[count + u] = 0
        row_ref[count + u] = 0
    for side, ref in ((0, left_ref), (1, right_ref)):
        for i, strip in enumerate(strip_pack(lat_ref, WIDTHS[0], side)):
            ref[i] = strip


def gather_latent(first, site_cells, lat_rows):
    sources, blocks, lanes = site_cells.shape
    rows, species, cols = lat_rows.shape
    room = sources * blocks + 2 * TURN
    strips = strip_counts(rows)[0]
    f32 = lambda *s: jax.ShapeDtypeStruct(s, F32)
    i32 = lambda *s: jax.ShapeDtypeStruct(s, jnp.int32)
    return pl.pallas_call(
        gather_kernel,
        in_specs=[whole(SMEM), whole(), whole()],
        out_specs=[whole()] * 2 + [whole(SMEM)] * 3 + [whole()] * 2,
        out_shape=[
            f32(room, species, lanes),
            i32(room, 1, lanes),
            i32(room),
            i32(room),
            i32(STAGES + 1),
            f32(strips, species, LANES),
            f32(strips, species, LANES),
        ],
        compiler_params=params(56),
        cost_estimate=cost(16 * room * lanes * species, 8 * room * lanes * species),
        name="gather_latent",
    )(first, site_cells, lat_rows)


def hi_lo(value):
    high = value.astype(BF16)
    low = (value - high.astype(F32)).astype(BF16)
    return high, low


def site_kernel(list_ref, row_ref, count_ref, cells_hbm, values_hbm, sites_hbm, lat_ref,
                g_ref, w_ref, left_ref, right_ref, up_ref, down_ref,
                cells_ref, values_ref, sites_ref, in_sem):
    rows, species, cols = g_ref.shape
    sources, _, slots = sites_ref.shape
    blocks = slots // SB
    tiles = cols // LANES
    loads = []
    for stage in range(STAGES):
        size = sources // STAGES
        last = stage == STAGES - 1
        spots = pl.ds(stage * size * blocks, size * blocks + (TURN if last else 0))
        for i, (src, dst, part) in enumerate((
            (sites_hbm, sites_ref, pl.ds(stage * size, size)),
            (values_hbm, values_ref, spots),
            (cells_hbm, cells_ref, spots),
        )):
            copy = pltpu.make_async_copy(src.at[part], dst.at[part], in_sem.at[3 * stage + i])
            copy.start()
            loads.append(copy)
    g_ref[...] = jnp.zeros_like(g_ref)
    w_ref[...] = jnp.zeros_like(w_ref)
    lane_of = lax.broadcasted_iota(jnp.int32, (LANES, SB), 0).astype(jnp.int16)
    one = jnp.ones((LANES, SB), BF16)
    zero = jnp.zeros((LANES, SB), BF16)
    zero16 = jnp.zeros((2 * species, SB), BF16)

    def place(at):
        block = list_ref[at]
        source = block // blocks
        spot = pl.ds(pl.multiple_of((block % blocks) * SB, SB), SB)
        cell = jnp.broadcast_to(cells_ref[at], (2 * species, SB))
        low = (cell & (LANES - 1)).astype(jnp.int16)
        high = jnp.where(cell < 0, -1, (cell // LANES) & (tiles - 1)).astype(jnp.int16)
        eta = values_ref[at] + sites_ref[source, :species, spot]
        ratio = sites_ref[source, species:, spot]
        e = jnp.exp(-eta)
        psi = 1.0 / (1.0 + e)
        ep = e * psi
        weight = ep * psi
        gradient = ep * (1.0 - ratio) / (1.0 + e * ratio)
        both_hi, both_lo = hi_lo(jnp.concatenate([weight, gradient], axis=0))
        hot = jnp.where(lane_of == jnp.concatenate([low] * (LANES // low.shape[0]), axis=0), one, zero)
        placed_hi = []
        placed_lo = []
        for t in range(tiles):
            here = high == t
            placed_hi.append(jnp.where(here, both_hi, zero16))
            placed_lo.append(jnp.where(here, both_lo, zero16))
        left = jnp.concatenate(
            [jnp.concatenate(placed_hi, axis=0), jnp.concatenate(placed_lo, axis=0)], axis=1
        )
        right = jnp.concatenate([hot, hot], axis=1)
        return lax.dot_general(left, right, (((1,), (1,)), ((), ())), preferred_element_type=F32)

    def turn(i, carry):
        at = [i * TURN + u for u in range(TURN)]
        for spot in at:
            placed = place(spot)
            row = row_ref[spot]
            for t in range(tiles):
                lanes = pl.ds(t * LANES, LANES)
                start = 2 * species * t
                w_ref[row, :, lanes] += placed[start:start + species]
                g_ref[row, :, lanes] += placed[start + species:start + 2 * species]
        return carry

    for stage in range(STAGES):
        for copy in loads[3 * stage:3 * stage + 3]:
            copy.wait()
        first = count_ref[stage] // TURN
        end = count_ref[stage + 1]
        if stage == STAGES - 1:
            end = end + TURN - 1
        lax.fori_loop(first, end // TURN, turn, 0)

    for side, ref in ((0, left_ref), (1, right_ref)):
        strips = strip_pack(g_ref, WIDTHS[1], side) + strip_pack(w_ref, WIDTHS[2], side)
        for i, strip in enumerate(strips):
            ref[i] = strip
    for ref, low_side in ((up_ref, True), (down_ref, False)):
        i = 0
        for field, depth in zip((lat_ref, g_ref, w_ref), DEPTHS):
            count = field.shape[0]
            for row in range(depth) if low_side else range(count - depth, count):
                for tile in load_row(field, row):
                    ref[i] = tile
                    i += 1
        for j in range(i, ref.shape[0]):
            ref[j] = jnp.zeros((species, LANES), F32)


def site_terms(blocks, sites, lat_edges, rows):
    values, cells, block_list, block_rows, count = blocks
    species, cols = lat_edges.shape[1:]
    counts = strip_counts(rows)
    strips = counts[1] + counts[2]
    edge_tiles = sum(DEPTHS) * (cols // LANES) + 2 * sum(counts)
    shape = lambda *s: jax.ShapeDtypeStruct(s, F32)
    return pl.pallas_call(
        site_kernel,
        in_specs=[whole(SMEM)] * 3 + [anywhere()] * 3 + [whole()],
        out_specs=[whole()] * 6,
        out_shape=[
            shape(rows, species, cols),
            shape(rows, species, cols),
            shape(strips, species, LANES),
            shape(strips, species, LANES),
            shape(edge_tiles, species, LANES),
            shape(edge_tiles, species, LANES),
        ],
        scratch_shapes=[
            VMEM(cells.shape, jnp.int32),
            VMEM(values.shape, F32),
            VMEM(sites.shape, F32),
            dma(3 * STAGES),
        ],
        compiler_params=params(50),
        name="site_terms",
    )(block_list, block_rows, count, cells, values, sites, lat_edges)


def krylov_kernel(edge_ref, ksq_ref, lat_ref, g_ref, w_ref, right_ref, left_ref, up_ref, down_ref,
                  b_out, h_out, h2_out, part_ref, lx, bx, wx, m_ref):
    rows, species, cols = g_ref.shape
    tiles = cols // LANES
    lane = lax.broadcasted_iota(jnp.int32, (species, LANES), 1)
    ksq = jnp.broadcast_to(ksq_ref[:, :1], (species, LANES))
    ksq4 = ksq + 4.0
    scale = 4.0 * math.pi * ksq
    edges = Edges(edge_ref, lane)
    halo = pl.ds(cols, LANES)
    counts = strip_counts(rows)
    exts = (lx, bx, wx)

    def strips(ref, base):
        out = []
        for count in counts:
            out.append([ref[base + i] for i in range(count)])
            base += count
        return out

    right = strips(right_ref, 0)
    left = strips(left_ref, 0)
    for field, ext, depth, width, r, l in zip((lat_ref, g_ref, w_ref), exts, DEPTHS, WIDTHS, right, left):
        ext[depth:rows + depth, :, :cols] = field[...]
        for row in range(rows):
            ext[depth + row, :, halo] = halo_tile(r, l, row, width, lane)
    for ref, above in ((up_ref, True), (down_ref, False)):
        base = sum(DEPTHS) * tiles
        right = strips(ref, base)
        left = strips(ref, base + sum(counts))
        i = 0
        for ext, depth, width, r, l in zip(exts, DEPTHS, WIDTHS, right, left):
            for row in range(depth):
                to = row if above else rows + depth + row
                came = rows - depth + row if above else row
                for t in range(tiles):
                    ext[to, :, t * LANES:(t + 1) * LANES] = ref[i]
                    i += 1
                ext[to, :, halo] = halo_tile(r, l, came, width, lane)

    def factor(src, src_pad, row, count=None):
        return factor_row(src, row + src_pad, ksq4, lane, count)

    def run(first, last, pad, row_tiles, dst):
        edges.pass_rows(first + pad, last + pad, pad, rows + pad, lambda r: row_tiles(r - pad), dst)

    run(-5, rows + 5, 5, lambda r: factor(lx, 6, r), m_ref)

    def right_side(r):
        return [g - scale * f for g, f in zip(load_row(bx, r + 4), factor(m_ref, 5, r))]

    run(-4, rows + 4, 4, right_side, bx)
    run(-3, rows + 3, 5, lambda r: factor(bx, 4, r), m_ref)

    def image(r):
        b = load_row(bx, r + 4)
        w = load_row(wx, r + 2)
        return [scale * f + x * y for f, x, y in zip(factor(m_ref, 5, r), w, b)]

    run(-2, rows + 2, 6, image, lx)
    run(-1, rows + 1, 5, lambda r: factor(lx, 6, r), m_ref)

    zero = jnp.zeros((species, LANES), F32)
    group = 8

    def sum_turn(i, sums):
        bb, bh, hh, hh2 = sums
        for u in range(group):
            row = i * group + u
            for t, f in enumerate(factor(m_ref, 5, row, tiles)):
                lanes = pl.ds(t * LANES, LANES)
                b = bx[row + 4, :, lanes]
                h = lx[row + 6, :, lanes]
                h2 = scale * f + wx[row + 2, :, lanes] * h
                b_out[row, :, lanes] = b
                h_out[row, :, lanes] = h
                h2_out[row, :, lanes] = h2
                bb = bb + b * b
                bh = bh + b * h
                hh = hh + h * h
                hh2 = hh2 + h * h2
        return bb, bh, hh, hh2

    sums = lax.fori_loop(0, rows // group, sum_turn, (zero, zero, zero, zero))
    lane_row = lax.broadcasted_iota(jnp.int32, part_ref.shape, 1)
    part = jnp.zeros(part_ref.shape, F32)
    for i, total in enumerate(sums):
        narrow = jnp.sum(total, axis=0, keepdims=True)
        narrow = jnp.sum(narrow, axis=1, keepdims=True)
        part = jnp.where(lane_row == i, narrow, part)
    part_ref[...] = part


def krylov(edges, ksq, lat_rows, g, w, right, left, from_up, from_down, devices):
    rows, species, cols = g.shape
    ext = lambda pad: (rows + 2 * pad, species, cols + LANES)
    shape = lambda *s: jax.ShapeDtypeStruct(s, F32)
    field = shape(rows, species, cols)
    return pl.pallas_call(
        krylov_kernel,
        in_specs=[whole(SMEM)] + [whole()] * 8,
        out_specs=[whole()] * 4,
        out_shape=[field, field, field, shape(devices, LANES)],
        scratch_shapes=[VMEM(ext(pad), F32) for pad in (6, 4, 2, 5)],
        compiler_params=params(20),
        name="krylov",
    )(edges, ksq, lat_rows, g, w, right, left, from_up, from_down)


def finish_kernel(parts_ref, b_ref, h_ref, h2_ref, step_ref, residual_ref):
    total = jnp.sum(parts_ref[...], axis=0, keepdims=True)
    lane = lax.broadcasted_iota(jnp.int32, total.shape, 1)

    def pick(i):
        return jnp.sum(jnp.where(lane == i, total, 0.0), axis=1, keepdims=True)

    bb, bh, hh, hh2 = (pick(i) for i in range(4))
    alpha = bb / bh
    rr = bb - 2.0 * alpha * bh + alpha * alpha * hh
    beta = rr / bb
    grown = 1.0 + beta
    curve = grown * grown * bh - 2.0 * grown * alpha * hh + alpha * alpha * hh2
    later = rr / curve
    c0 = (alpha + later * grown)[None]
    c1 = (later * alpha)[None]
    b = b_ref[...]
    h = h_ref[...]
    step_ref[...] = jnp.swapaxes(c0 * b - c1 * h, 0, 1)
    residual_ref[...] = jnp.swapaxes(b - c0 * h + c1 * h2_ref[...], 0, 1)


def finish(parts, b, h, h2):
    rows, species, cols = b.shape
    group = 16
    field = pl.BlockSpec((group, species, cols), lambda i: (i, 0, 0))
    out = pl.BlockSpec((species, group, cols), lambda i: (0, i, 0))
    shape = jax.ShapeDtypeStruct((species, rows, cols), F32)
    return pl.pallas_call(
        finish_kernel,
        grid=(rows // group,),
        in_specs=[pl.BlockSpec(parts.shape, lambda i: (0, 0)), field, field, field],
        out_specs=[out, out],
        out_shape=[shape, shape],
        compiler_params=params(24),
        name="finish",
    )(parts, b, h, h2)


def neighbour_pairs(count):
    forward = [(i, i + 1) for i in range(count - 1)]
    backward = [(target, source) for source, target in forward]
    return forward, backward


def per_device(latent, site_offset, site_counts, site_cells, detect_prob, kappa_sq):
    species, rows, cols = latent.shape
    n_gr, n_gc = lax.axis_size("gr"), lax.axis_size("gc")
    gr, gc = lax.axis_index("gr"), lax.axis_index("gc")
    down_pairs, up_pairs = neighbour_pairs(n_gr)
    right_pairs, left_pairs = neighbour_pairs(n_gc)
    sites = lax.all_to_all(
        pack_sites(site_offset, site_counts, detect_prob), MESH, split_axis=0, concat_axis=0, tiled=True
    )
    edges = jnp.stack([gr > 0, gr < n_gr - 1, gc > 0, gc < n_gc - 1]).astype(jnp.int32)
    ksq = jnp.broadcast_to(kappa_sq[:, None], (species, LANES))
    lat_rows = jnp.transpose(latent, (1, 0, 2))
    depth = DEPTHS[0]
    lat_edges = jnp.concatenate([lat_rows[:depth], lat_rows[-depth:]], axis=0)
    first = site_cells[:, ::SB].reshape(-1)
    site_cells = site_cells.reshape(site_cells.shape[0], -1, SB)
    *blocks, lat_left, lat_right = gather_latent(first, site_cells, lat_rows)

    g, w, to_left, to_right, to_up, to_down = site_terms(blocks, sites, lat_edges, rows)
    from_left = lax.ppermute(jnp.concatenate([lat_right, to_right], axis=0), "gc", right_pairs)
    from_right = lax.ppermute(jnp.concatenate([lat_left, to_left], axis=0), "gc", left_pairs)
    strips = jnp.concatenate([from_right, from_left], axis=0)
    spot = (to_up.shape[0] - strips.shape[0], 0, 0)
    to_up = lax.dynamic_update_slice(to_up, strips, spot)
    to_down = lax.dynamic_update_slice(to_down, strips, spot)
    from_up = lax.ppermute(to_down, "gr", down_pairs)
    from_down = lax.ppermute(to_up, "gr", up_pairs)

    b, h, h2, part = krylov(edges, ksq, lat_rows, g, w, from_right, from_left, from_up, from_down, n_gr * n_gc)
    parts = lax.all_to_all(part, MESH, split_axis=0, concat_axis=0, tiled=True)
    return finish(parts, b, h, h2)


def solution(mesh):
    in_specs = (
        P(None, "gr", "gc"),
        P(None, ("gr", "gc"), None),
        P(None, ("gr", "gc"), None),
        P(("gr", "gc"), None),
        P(),
        P(),
    )
    out_specs = (P(None, "gr", "gc"), P(None, "gr", "gc"))
    return jax.shard_map(
        per_device, mesh=mesh, in_specs=in_specs, out_specs=out_specs, check_vma=False
    )
```

```python
import functools
import math

import jax
import jax.numpy as jnp
from jax import lax
from jax.experimental import pallas as pl
from jax.experimental.pallas import tpu as pltpu
from jax.sharding import PartitionSpec as P

SB = 128
VISITS = 4
LANES = 128
MESH = ("gr", "gc")
VMEM = pltpu.VMEM
SMEM = pltpu.SMEM
F32 = jnp.float32
BF16 = jnp.bfloat16


def whole(space=VMEM):
    return pl.BlockSpec(memory_space=space)


def params(mib):
    return pltpu.CompilerParams(vmem_limit_bytes=mib * 1024 * 1024)


def anywhere():
    return pl.BlockSpec(memory_space=pl.ANY)


def dma(count):
    return pltpu.SemaphoreType.DMA((count,))


def cost(flops, moved):
    return pl.CostEstimate(flops=flops, bytes_accessed=moved, transcendentals=0)


def per_species(ref):
    species = ref.shape[0]
    row = lax.broadcasted_iota(jnp.int32, (species, LANES), 0)
    out = jnp.zeros((species, LANES), F32)
    for k in range(species):
        out = jnp.where(row == k, ref[k], out)
    return out


def pack_kernel(prob_ref, offset_hbm, counts_hbm, out_hbm, offset, counts, out, in_sem, out_sem):
    species, owners, slots = offset.shape
    pieces = in_sem.shape[0] // 2
    size = owners // pieces
    loads = []
    for p in range(pieces):
        part = pl.ds(p * size, size)
        for i, (src, dst) in enumerate(((offset_hbm, offset), (counts_hbm, counts))):
            copy = pltpu.make_async_copy(src.at[:, part], dst.at[:, part], in_sem.at[2 * p + i])
            copy.start()
            loads.append(copy)
    prob = per_species(prob_ref)
    square = (1.0 - prob) * (1.0 - prob)
    q = (1.0 / (square * square))[None]
    group = 8
    stores = []
    for p in range(pieces):
        loads[2 * p].wait()
        loads[2 * p + 1].wait()

        def turn(i, carry):
            rows = pl.ds(pl.multiple_of(p * size + i * group, group), group)
            for t in range(slots // LANES):
                lanes = pl.ds(t * LANES, LANES)
                offsets = jnp.swapaxes(offset[:, rows, lanes], 0, 1)
                found = jnp.swapaxes(counts[:, rows, lanes], 0, 1)
                out[rows, :species, lanes] = offsets
                out[rows, species:, lanes] = jnp.where(found > 0, jnp.zeros_like(offsets), q)
            return carry

        lax.fori_loop(0, size // group, turn, 0)
        part = pl.ds(p * size, size)
        copy = pltpu.make_async_copy(out.at[part], out_hbm.at[part], out_sem.at[p])
        copy.start()
        stores.append(copy)
    for copy in stores:
        copy.wait()


def pack_sites(site_offset, site_counts, detect_prob):
    species, owners, slots = site_offset.shape
    pieces = 4
    return pl.pallas_call(
        pack_kernel,
        in_specs=[whole(SMEM), anywhere(), anywhere()],
        out_specs=anywhere(),
        out_shape=jax.ShapeDtypeStruct((owners, 2 * species, slots), F32),
        scratch_shapes=[
            VMEM(site_offset.shape, F32),
            VMEM(site_offset.shape, jnp.int32),
            VMEM((owners, 2 * species, slots), F32),
            dma(2 * pieces),
            dma(pieces),
        ],
        compiler_params=params(56),
        name="pack_sites",
    )(detect_prob, site_offset, site_counts)


def load_row(ref, row):
    return [ref[row, :, t * LANES:(t + 1) * LANES] for t in range(ref.shape[2] // LANES)]


def store_row(ref, row, tiles):
    for t, tile in enumerate(tiles):
        ref[row, :, t * LANES:(t + 1) * LANES] = tile


def factor_row(ref, row, ksq4, lane, count=None):
    center = load_row(ref, row)
    above = load_row(ref, row - 1)
    below = load_row(ref, row + 1)
    total = len(center)
    right = [pltpu.roll(tile, 1, 1) for tile in center]
    left = [pltpu.roll(tile, LANES - 1, 1) for tile in center]
    out = []
    for t in range(count or total):
        from_left = jnp.where(lane == 0, right[t - 1], right[t])
        from_right = jnp.where(lane == LANES - 1, left[(t + 1) % total], left[t])
        out.append(ksq4 * center[t] - ((above[t] + below[t]) + (from_left + from_right)))
    return out


def each_row(first, last, body, chunk=16):
    turns = (last - first) // chunk

    def turn(i, carry):
        for u in range(chunk):
            body(first + i * chunk + u)
        return carry

    lax.fori_loop(0, turns, turn, 0)
    for row in range(first + turns * chunk, last):
        body(row)


class Edges:
    def __init__(self, lane):
        gr, gc = lax.axis_index("gr"), lax.axis_index("gc")
        self.up, self.down, left, right = (
            jnp.where(there, jnp.float32(1.0), jnp.float32(0.0))
            for there in (
                gr > 0,
                gr < lax.axis_size("gr") - 1,
                gc > 0,
                gc < lax.axis_size("gc") - 1,
            )
        )
        self.halo = jnp.where(lane < LANES // 2, right, left)

    def pass_rows(self, first, last, low, high, row_tiles, dst_ref):
        def put(row, scale):
            tiles = row_tiles(row)
            tiles[-1] = tiles[-1] * self.halo
            if scale is not None:
                tiles = [tile * scale for tile in tiles]
            store_row(dst_ref, row, tiles)

        for row in range(first, low):
            put(row, self.up)
        each_row(low, high, lambda row: put(row, None))
        for row in range(high, last):
            put(row, self.down)


def strip_pack(field_ref, width, side):
    rows, species, cols = field_ref.shape
    per_tile = LANES // width
    lane = lax.broadcasted_iota(jnp.int32, (species, LANES), 1) // width
    tiles = []
    for tile in range(rows // per_tile):
        packed = jnp.zeros((species, LANES), F32)
        for p in range(per_tile):
            row = tile * per_tile + p
            if side == 0:
                part = field_ref[row, :, :LANES]
                shift = (p * width) % LANES
            else:
                part = field_ref[row, :, cols - LANES:]
                shift = (p * width + width) % LANES
            if shift:
                part = pltpu.roll(part, shift, 1)
            packed = jnp.where(lane == p, part, packed)
        tiles.append(packed)
    return tiles


def halo_tile(right_tiles, left_tiles, row, width, lane):
    per_tile = LANES // width
    tile, p = row // per_tile, row % per_tile
    shift = (LANES - p * width) % LANES
    from_right = pltpu.roll(right_tiles[tile], shift, 1) if shift else right_tiles[tile]
    shift = (LANES - p * width - width) % LANES
    from_left = pltpu.roll(left_tiles[tile], shift, 1) if shift else left_tiles[tile]
    return jnp.where(lane < width, from_right, jnp.where(lane >= LANES - width, from_left, 0.0))


WIDTHS = (8, 4, 2)
DEPTHS = (6, 4, 2)
TURN = 32
STAGES = 4
LIST = 8


def strip_counts(rows):
    return [rows * width // LANES for width in WIDTHS]


def gather_kernel(first_ref, cells_ref, lat_ref, values_ref, cells_out, list_ref, halo_ref):
    sources, blocks = cells_ref.shape[:2]
    rows, species, cols = lat_ref.shape
    tiles = cols // LANES
    total = sources * blocks
    per_stage = sources // STAGES

    def step(source, spot):
        for j in range(blocks):
            cell = cells_ref[source, j:j + 1, :]
            first = first_ref[source * blocks + j]
            row = jnp.maximum(first, 0) // cols
            live = first >= 0
            at = jnp.where(live, spot, total + TURN)
            wide = jnp.broadcast_to(cell, (species, SB))
            low = wide & (LANES - 1)
            high = (wide // LANES) & (tiles - 1)
            value = jnp.zeros((species, SB), F32)
            for t in range(tiles):
                part = lat_ref[row, :, t * LANES:(t + 1) * LANES]
                picked = jnp.take_along_axis(part, low, axis=1)
                value = jnp.where(high == t, picked, value)
            values_ref[at] = value
            cells_out[at] = wide
            list_ref[LIST + at] = (source * blocks + j) * rows + row
            spot = spot + live.astype(jnp.int32)
        return spot

    count = jnp.int32(0)
    for stage in range(STAGES):
        list_ref[stage] = count
        count = lax.fori_loop(stage * per_stage, (stage + 1) * per_stage, step, count)
    list_ref[STAGES] = count
    for u in range(TURN):
        values_ref[count + u] = jnp.zeros((species, SB), F32)
        cells_out[count + u] = jnp.full((species, SB), -1, jnp.int32)
        list_ref[LIST + count + u] = 0
    depth = DEPTHS[0]
    edges = strip_pack(lat_ref, WIDTHS[0], 0) + strip_pack(lat_ref, WIDTHS[0], 1)
    for row in list(range(depth)) + list(range(rows - depth, rows)):
        edges += load_row(lat_ref, row)
    for i, tile in enumerate(edges):
        halo_ref[i] = tile


def gather_latent(first, site_cells, lat_rows):
    sources, blocks, lanes = site_cells.shape
    rows, species, cols = lat_rows.shape
    room = sources * blocks + 2 * TURN
    strips = strip_counts(rows)[0]
    f32 = lambda *s: jax.ShapeDtypeStruct(s, F32)
    i32 = lambda *s: jax.ShapeDtypeStruct(s, jnp.int32)
    return pl.pallas_call(
        gather_kernel,
        in_specs=[whole(SMEM), whole(), whole()],
        out_specs=[whole()] * 2 + [whole(SMEM), whole()],
        out_shape=[
            f32(room, species, lanes),
            i32(room, species, lanes),
            i32(LIST + room),
            f32(2 * strips + 2 * DEPTHS[0] * (cols // LANES), species, LANES),
        ],
        compiler_params=params(56),
        cost_estimate=cost(16 * room * lanes * species, 8 * room * lanes * species),
        name="gather_latent",
    )(first, site_cells, lat_rows)


def hi_lo(value):
    high = value.astype(BF16)
    low = (value - high.astype(F32)).astype(BF16)
    return high, low


def site_kernel(list_ref, cells_hbm, values_hbm, sites_hbm, lat_ref,
                g_ref, w_ref, left_ref, right_ref, up_ref, down_ref,
                cells_ref, values_ref, sites_ref, in_sem):
    rows, species, cols = g_ref.shape
    sources, _, slots = sites_ref.shape
    blocks = slots // SB
    tiles = cols // LANES
    loads = []
    for stage in range(STAGES):
        size = sources // STAGES
        last = stage == STAGES - 1
        spots = pl.ds(stage * size * blocks, size * blocks + (TURN if last else 0))
        for i, (src, dst, part) in enumerate((
            (sites_hbm, sites_ref, pl.ds(stage * size, size)),
            (values_hbm, values_ref, spots),
            (cells_hbm, cells_ref, spots),
        )):
            copy = pltpu.make_async_copy(src.at[part], dst.at[part], in_sem.at[3 * stage + i])
            copy.start()
            loads.append(copy)
    g_ref[...] = jnp.zeros_like(g_ref)
    w_ref[...] = jnp.zeros_like(w_ref)
    lane_of = lax.broadcasted_iota(jnp.int32, (LANES, SB), 0).astype(jnp.int16)
    one = jnp.ones((LANES, SB), BF16)
    zero = jnp.zeros((LANES, SB), BF16)
    zero16 = jnp.zeros((2 * species, SB), BF16)

    def place(at):
        block = list_ref[LIST + at] // rows
        source = block // blocks
        spot = pl.ds(pl.multiple_of((block % blocks) * SB, SB), SB)
        cell = jnp.concatenate([cells_ref[at]] * 2, axis=0)
        low = (cell & (LANES - 1)).astype(jnp.int16)
        high = jnp.where(cell < 0, -1, (cell // LANES) & (tiles - 1)).astype(jnp.int16)
        eta = values_ref[at] + sites_ref[source, :species, spot]
        ratio = sites_ref[source, species:, spot]
        e = jnp.exp(-eta)
        psi = 1.0 / (1.0 + e)
        ep = e * psi
        weight = ep * psi
        gradient = ep * (1.0 - ratio) / (1.0 + e * ratio)
        both_hi, both_lo = hi_lo(jnp.concatenate([weight, gradient], axis=0))
        hot = jnp.where(lane_of == jnp.concatenate([low] * (LANES // low.shape[0]), axis=0), one, zero)
        placed_hi = []
        placed_lo = []
        for t in range(tiles):
            here = high == t
            placed_hi.append(jnp.where(here, both_hi, zero16))
            placed_lo.append(jnp.where(here, both_lo, zero16))
        left = jnp.concatenate(
            [jnp.concatenate(placed_hi, axis=0), jnp.concatenate(placed_lo, axis=0)], axis=1
        )
        right = jnp.concatenate([hot, hot], axis=1)
        return lax.dot_general(left, right, (((1,), (1,)), ((), ())), preferred_element_type=F32)

    def turn(i, carry):
        at = [i * TURN + u for u in range(TURN)]
        for spot in at:
            placed = place(spot)
            row = list_ref[LIST + spot] % rows
            for t in range(tiles):
                lanes = pl.ds(t * LANES, LANES)
                start = 2 * species * t
                w_ref[row, :, lanes] += placed[start:start + species]
                g_ref[row, :, lanes] += placed[start + species:start + 2 * species]
        return carry

    for stage in range(STAGES):
        for copy in loads[3 * stage:3 * stage + 3]:
            copy.wait()
        first = list_ref[stage] // TURN
        end = list_ref[stage + 1]
        if stage == STAGES - 1:
            end = end + TURN - 1
        lax.fori_loop(first, end // TURN, turn, 0)

    lat_strips = strip_counts(rows)[0]
    for side, ref in ((0, left_ref), (1, right_ref)):
        strips = [lat_ref[side * lat_strips + i] for i in range(lat_strips)]
        strips += strip_pack(g_ref, WIDTHS[1], side) + strip_pack(w_ref, WIDTHS[2], side)
        for i, strip in enumerate(strips):
            ref[i] = strip
    for ref, low_side in ((up_ref, True), (down_ref, False)):
        i = DEPTHS[0] * tiles
        base = 2 * lat_strips + (0 if low_side else i)
        for t in range(i):
            ref[t] = lat_ref[base + t]
        for field, depth in zip((g_ref, w_ref), DEPTHS[1:]):
            for row in range(depth) if low_side else range(rows - depth, rows):
                for tile in load_row(field, row):
                    ref[i] = tile
                    i += 1
        for j in range(i, ref.shape[0]):
            ref[j] = jnp.zeros((species, LANES), F32)


def site_terms(values, cells, block_list, halo, sites, rows, cols):
    species = values.shape[1]
    counts = strip_counts(rows)
    strips = sum(counts)
    edge_tiles = sum(DEPTHS) * (cols // LANES) + 2 * sum(counts)
    shape = lambda *s: jax.ShapeDtypeStruct(s, F32)
    return pl.pallas_call(
        site_kernel,
        in_specs=[whole(SMEM)] + [anywhere()] * 3 + [whole()],
        out_specs=[whole()] * 6,
        out_shape=[
            shape(rows, species, cols),
            shape(rows, species, cols),
            shape(strips, species, LANES),
            shape(strips, species, LANES),
            shape(edge_tiles, species, LANES),
            shape(edge_tiles, species, LANES),
        ],
        scratch_shapes=[
            VMEM(cells.shape, jnp.int32),
            VMEM(values.shape, F32),
            VMEM(sites.shape, F32),
            dma(3 * STAGES),
        ],
        compiler_params=params(48),
        name="site_terms",
    )(block_list, cells, values, sites, halo)


def krylov_kernel(ksq_ref, lat_ref, g_ref, w_ref, right_ref, left_ref, up_ref, down_ref,
                  b_out, h_out, h2_out, part_ref, lx, bx, wx, m_ref):
    rows, species, cols = g_ref.shape
    tiles = cols // LANES
    lane = lax.broadcasted_iota(jnp.int32, (species, LANES), 1)
    ksq = per_species(ksq_ref)
    ksq4 = ksq + 4.0
    scale = 4.0 * math.pi * ksq
    edges = Edges(lane)
    halo = pl.ds(cols, LANES)
    counts = strip_counts(rows)
    exts = (lx, bx, wx)

    def strips(ref, base):
        out = []
        for count in counts:
            out.append([ref[base + i] for i in range(count)])
            base += count
        return out

    right = strips(right_ref, 0)
    left = strips(left_ref, 0)
    for field, ext, depth, width, r, l in zip((lat_ref, g_ref, w_ref), exts, DEPTHS, WIDTHS, right, left):
        ext[depth:rows + depth, :, :cols] = field[...]
        for row in range(rows):
            ext[depth + row, :, halo] = halo_tile(r, l, row, width, lane)
    for ref, above in ((up_ref, True), (down_ref, False)):
        base = sum(DEPTHS) * tiles
        right = strips(ref, base)
        left = strips(ref, base + sum(counts))
        i = 0
        for ext, depth, width, r, l in zip(exts, DEPTHS, WIDTHS, right, left):
            for row in range(depth):
                to = row if above else rows + depth + row
                came = rows - depth + row if above else row
                for t in range(tiles):
                    ext[to, :, t * LANES:(t + 1) * LANES] = ref[i]
                    i += 1
                ext[to, :, halo] = halo_tile(r, l, came, width, lane)

    def factor(src, src_pad, row, count=None):
        return factor_row(src, row + src_pad, ksq4, lane, count)

    def run(first, last, pad, row_tiles, dst):
        edges.pass_rows(first + pad, last + pad, pad, rows + pad, lambda r: row_tiles(r - pad), dst)

    run(-5, rows + 5, 5, lambda r: factor(lx, 6, r), m_ref)

    def right_side(r):
        return [g - scale * f for g, f in zip(load_row(bx, r + 4), factor(m_ref, 5, r))]

    run(-4, rows + 4, 4, right_side, bx)
    run(-3, rows + 3, 5, lambda r: factor(bx, 4, r), m_ref)

    def image(r):
        b = load_row(bx, r + 4)
        w = load_row(wx, r + 2)
        return [scale * f + x * y for f, x, y in zip(factor(m_ref, 5, r), w, b)]

    run(-2, rows + 2, 6, image, lx)
    run(-1, rows + 1, 5, lambda r: factor(lx, 6, r), m_ref)

    zero = jnp.zeros((species, LANES), F32)
    group = 8

    def sum_turn(i, sums):
        bb, bh, hh, hh2 = sums
        for u in range(group):
            row = i * group + u
            for t, f in enumerate(factor(m_ref, 5, row, tiles)):
                lanes = pl.ds(t * LANES, LANES)
                b = bx[row + 4, :, lanes]
                h = lx[row + 6, :, lanes]
                h2 = scale * f + wx[row + 2, :, lanes] * h
                b_out[row, :, lanes] = b
                h_out[row, :, lanes] = h
                h2_out[row, :, lanes] = h2
                bb = bb + b * b
                bh = bh + b * h
                hh = hh + h * h
                hh2 = hh2 + h * h2
        return bb, bh, hh, hh2

    sums = lax.fori_loop(0, rows // group, sum_turn, (zero, zero, zero, zero))
    lane_row = lax.broadcasted_iota(jnp.int32, part_ref.shape, 1)
    part = jnp.zeros(part_ref.shape, F32)
    for i, total in enumerate(sums):
        narrow = jnp.sum(total, axis=0, keepdims=True)
        narrow = jnp.sum(narrow, axis=1, keepdims=True)
        part = jnp.where(lane_row == i, narrow, part)
    part_ref[...] = part


def krylov(ksq, lat_rows, g, w, right, left, from_up, from_down, devices):
    rows, species, cols = g.shape
    ext = lambda pad: (rows + 2 * pad, species, cols + LANES)
    shape = lambda *s: jax.ShapeDtypeStruct(s, F32)
    field = shape(rows, species, cols)
    return pl.pallas_call(
        krylov_kernel,
        in_specs=[whole(SMEM)] + [whole()] * 7,
        out_specs=[whole()] * 4,
        out_shape=[field, field, field, shape(devices, LANES)],
        scratch_shapes=[VMEM(ext(pad), F32) for pad in (6, 4, 2, 5)],
        compiler_params=params(20),
        name="krylov",
    )(ksq, lat_rows, g, w, right, left, from_up, from_down)


def finish_kernel(parts_ref, b_ref, h_ref, h2_ref, step_ref, residual_ref):
    total = jnp.sum(parts_ref[...], axis=0, keepdims=True)
    lane = lax.broadcasted_iota(jnp.int32, total.shape, 1)

    def pick(i):
        return jnp.sum(jnp.where(lane == i, total, 0.0), axis=1, keepdims=True)

    bb, bh, hh, hh2 = (pick(i) for i in range(4))
    alpha = bb / bh
    rr = bb - 2.0 * alpha * bh + alpha * alpha * hh
    beta = rr / bb
    grown = 1.0 + beta
    curve = grown * grown * bh - 2.0 * grown * alpha * hh + alpha * alpha * hh2
    later = rr / curve
    c0 = (alpha + later * grown)[None]
    c1 = (later * alpha)[None]
    b = b_ref[...]
    h = h_ref[...]
    step_ref[...] = jnp.swapaxes(c0 * b - c1 * h, 0, 1)
    residual_ref[...] = jnp.swapaxes(b - c0 * h + c1 * h2_ref[...], 0, 1)


def finish(parts, b, h, h2):
    rows, species, cols = b.shape
    group = 16
    field = pl.BlockSpec((group, species, cols), lambda i: (i, 0, 0))
    out = pl.BlockSpec((species, group, cols), lambda i: (0, i, 0))
    shape = jax.ShapeDtypeStruct((species, rows, cols), F32)
    return pl.pallas_call(
        finish_kernel,
        grid=(rows // group,),
        in_specs=[pl.BlockSpec(parts.shape, lambda i: (0, 0)), field, field, field],
        out_specs=[out, out],
        out_shape=[shape, shape],
        compiler_params=params(24),
        name="finish",
    )(parts, b, h, h2)


def neighbour_pairs(count):
    forward = [(i, i + 1) for i in range(count - 1)]
    backward = [(target, source) for source, target in forward]
    return forward, backward


def per_device(latent, site_offset, site_counts, site_cells, detect_prob, kappa_sq):
    species, rows, cols = latent.shape
    n_gr, n_gc = lax.axis_size("gr"), lax.axis_size("gc")
    down_pairs, up_pairs = neighbour_pairs(n_gr)
    right_pairs, left_pairs = neighbour_pairs(n_gc)
    sites = lax.all_to_all(
        pack_sites(site_offset, site_counts, detect_prob), MESH, split_axis=0, concat_axis=0, tiled=True
    )
    lat_rows = jnp.transpose(latent, (1, 0, 2))
    first = site_cells[:, ::SB].reshape(-1)
    site_cells = site_cells.reshape(site_cells.shape[0], -1, SB)
    blocks = gather_latent(first, site_cells, lat_rows)

    g, w, to_left, to_right, to_up, to_down = site_terms(*blocks, sites, rows, cols)
    from_left = lax.ppermute(to_right, "gc", right_pairs)
    from_right = lax.ppermute(to_left, "gc", left_pairs)
    strips = jnp.concatenate([from_right, from_left], axis=0)
    spot = (to_up.shape[0] - strips.shape[0], 0, 0)
    to_up = lax.dynamic_update_slice(to_up, strips, spot)
    to_down = lax.dynamic_update_slice(to_down, strips, spot)
    from_up = lax.ppermute(to_down, "gr", down_pairs)
    from_down = lax.ppermute(to_up, "gr", up_pairs)

    b, h, h2, part = krylov(kappa_sq, lat_rows, g, w, from_right, from_left, from_up, from_down, n_gr * n_gc)
    parts = lax.all_to_all(part, MESH, split_axis=0, concat_axis=0, tiled=True)
    return finish(parts, b, h, h2)


def solution(mesh):
    in_specs = (
        P(None, "gr", "gc"),
        P(None, ("gr", "gc"), None),
        P(None, ("gr", "gc"), None),
        P(("gr", "gc"), None),
        P(),
        P(),
    )
    out_specs = (P(None, "gr", "gc"), P(None, "gr", "gc"))
    return jax.shard_map(
        per_device, mesh=mesh, in_specs=in_specs, out_specs=out_specs, check_vma=False
    )
```

```python
import functools
import math

import jax
import jax.numpy as jnp
from jax import lax
from jax.experimental import pallas as pl
from jax.experimental.pallas import tpu as pltpu
from jax.sharding import PartitionSpec as P

SB = 128
VISITS = 4
LANES = 128
MESH = ("gr", "gc")
VMEM = pltpu.VMEM
SMEM = pltpu.SMEM
F32 = jnp.float32
BF16 = jnp.bfloat16


def whole(space=VMEM):
    return pl.BlockSpec(memory_space=space)


def params(mib):
    return pltpu.CompilerParams(vmem_limit_bytes=mib * 1024 * 1024)


def in_hbm():
    return pl.BlockSpec(memory_space=pltpu.HBM)


def dma(count):
    return pltpu.SemaphoreType.DMA((count,))


def cost(flops, moved):
    return pl.CostEstimate(flops=flops, bytes_accessed=moved, transcendentals=0)


def per_species(ref):
    species = ref.shape[0]
    row = lax.broadcasted_iota(jnp.int32, (species, LANES), 0)
    out = jnp.zeros((species, LANES), F32)
    for k in range(species):
        out = jnp.where(row == k, ref[k], out)
    return out


def pack_kernel(prob_ref, offset_hbm, counts_hbm, out_hbm, offset, counts, out, in_sem, out_sem):
    species, owners, slots = offset.shape
    pieces = in_sem.shape[0] // 2
    size = owners // pieces
    loads = []
    for p in range(pieces):
        part = pl.ds(p * size, size)
        for i, (src, dst) in enumerate(((offset_hbm, offset), (counts_hbm, counts))):
            copy = pltpu.make_async_copy(src.at[:, part], dst.at[:, part], in_sem.at[2 * p + i])
            copy.start()
            loads.append(copy)
    prob = per_species(prob_ref)
    square = (1.0 - prob) * (1.0 - prob)
    q = (1.0 / (square * square))[None]
    group = 8
    stores = []
    for p in range(pieces):
        loads[2 * p].wait()
        loads[2 * p + 1].wait()

        def turn(i, carry):
            rows = pl.ds(pl.multiple_of(p * size + i * group, group), group)
            for t in range(slots // LANES):
                lanes = pl.ds(t * LANES, LANES)
                offsets = jnp.swapaxes(offset[:, rows, lanes], 0, 1)
                found = jnp.swapaxes(counts[:, rows, lanes], 0, 1)
                out[rows, :species, lanes] = offsets
                out[rows, species:, lanes] = jnp.where(found > 0, jnp.zeros_like(offsets), q)
            return carry

        lax.fori_loop(0, size // group, turn, 0)
        part = pl.ds(p * size, size)
        copy = pltpu.make_async_copy(out.at[part], out_hbm.at[part], out_sem.at[p])
        copy.start()
        stores.append(copy)
    for copy in stores:
        copy.wait()


def pack_sites(site_offset, site_counts, detect_prob):
    species, owners, slots = site_offset.shape
    pieces = 8
    return pl.pallas_call(
        pack_kernel,
        in_specs=[whole(SMEM), in_hbm(), in_hbm()],
        out_specs=in_hbm(),
        out_shape=jax.ShapeDtypeStruct((owners, 2 * species, slots), F32),
        scratch_shapes=[
            VMEM(site_offset.shape, F32),
            VMEM(site_offset.shape, jnp.int32),
            VMEM((owners, 2 * species, slots), F32),
            dma(2 * pieces),
            dma(pieces),
        ],
        compiler_params=params(56),
        name="pack_sites",
    )(detect_prob, site_offset, site_counts)


def load_row(ref, row):
    return [ref[row, :, t * LANES:(t + 1) * LANES] for t in range(ref.shape[2] // LANES)]


def store_row(ref, row, tiles):
    for t, tile in enumerate(tiles):
        ref[row, :, t * LANES:(t + 1) * LANES] = tile


def factor_row(ref, row, ksq4, lane, count=None):
    center = load_row(ref, row)
    above = load_row(ref, row - 1)
    below = load_row(ref, row + 1)
    total = len(center)
    right = [pltpu.roll(tile, 1, 1) for tile in center]
    left = [pltpu.roll(tile, LANES - 1, 1) for tile in center]
    out = []
    for t in range(count or total):
        from_left = jnp.where(lane == 0, right[t - 1], right[t])
        from_right = jnp.where(lane == LANES - 1, left[(t + 1) % total], left[t])
        out.append(ksq4 * center[t] - ((above[t] + below[t]) + (from_left + from_right)))
    return out


def each_row(first, last, body, chunk=32):
    turns = (last - first) // chunk

    def turn(i, carry):
        for u in range(chunk):
            body(first + i * chunk + u)
        return carry

    lax.fori_loop(0, turns, turn, 0)
    for row in range(first + turns * chunk, last):
        body(row)


class Edges:
    def __init__(self, lane):
        gr, gc = lax.axis_index("gr"), lax.axis_index("gc")
        self.up, self.down, left, right = (
            jnp.where(there, jnp.float32(1.0), jnp.float32(0.0))
            for there in (
                gr > 0,
                gr < lax.axis_size("gr") - 1,
                gc > 0,
                gc < lax.axis_size("gc") - 1,
            )
        )
        self.halo = jnp.where(lane < LANES // 2, right, left)

    def pass_rows(self, first, last, low, high, row_tiles, dst_ref):
        def put(row, scale):
            tiles = row_tiles(row)
            tiles[-1] = tiles[-1] * self.halo
            if scale is not None:
                tiles = [tile * scale for tile in tiles]
            store_row(dst_ref, row, tiles)

        for row in range(first, low):
            put(row, self.up)
        each_row(low, high, lambda row: put(row, None))
        for row in range(high, last):
            put(row, self.down)


def strip_pack(field_ref, width, side):
    rows, species, cols = field_ref.shape
    per_tile = LANES // width
    lane = lax.broadcasted_iota(jnp.int32, (species, LANES), 1) // width
    tiles = []
    for tile in range(rows // per_tile):
        packed = jnp.zeros((species, LANES), F32)
        for p in range(per_tile):
            row = tile * per_tile + p
            if side == 0:
                part = field_ref[row, :, :LANES]
                shift = (p * width) % LANES
            else:
                part = field_ref[row, :, cols - LANES:]
                shift = (p * width + width) % LANES
            if shift:
                part = pltpu.roll(part, shift, 1)
            packed = jnp.where(lane == p, part, packed)
        tiles.append(packed)
    return tiles


def halo_tile(right_tiles, left_tiles, row, width, lane):
    per_tile = LANES // width
    tile, p = row // per_tile, row % per_tile
    shift = (LANES - p * width) % LANES
    from_right = pltpu.roll(right_tiles[tile], shift, 1) if shift else right_tiles[tile]
    shift = (LANES - p * width - width) % LANES
    from_left = pltpu.roll(left_tiles[tile], shift, 1) if shift else left_tiles[tile]
    return jnp.where(lane < width, from_right, jnp.where(lane >= LANES - width, from_left, 0.0))


WIDTHS = (8, 4, 2)
DEPTHS = (6, 4, 2)
TURN = 32
STAGES = 4
LIST = 8


def strip_counts(rows):
    return [rows * width // LANES for width in WIDTHS]


def gather_kernel(first_ref, cells_ref, lat_ref, values_ref, cells_out, list_ref):
    sources, blocks = cells_ref.shape[:2]
    rows, species, cols = lat_ref.shape
    tiles = cols // LANES
    total = sources * blocks
    per_stage = sources // STAGES

    def step(source, spot):
        for j in range(blocks):
            cell = cells_ref[source, j:j + 1, :]
            first = first_ref[source * blocks + j]
            row = jnp.maximum(first, 0) // cols
            live = first >= 0
            at = jnp.where(live, spot, total + TURN)
            wide = jnp.broadcast_to(cell, (species, SB))
            low = wide & (LANES - 1)
            high = (wide // LANES) & (tiles - 1)
            value = jnp.zeros((species, SB), F32)
            for t in range(tiles):
                part = lat_ref[row, :, t * LANES:(t + 1) * LANES]
                picked = jnp.take_along_axis(part, low, axis=1)
                value = jnp.where(high == t, picked, value)
            values_ref[at] = value
            cells_out[at] = wide
            list_ref[LIST + at] = (source * blocks + j) * rows + row
            spot = spot + live.astype(jnp.int32)
        return spot

    count = jnp.int32(0)
    for stage in range(STAGES):
        list_ref[stage] = count
        count = lax.fori_loop(stage * per_stage, (stage + 1) * per_stage, step, count)
    list_ref[STAGES] = count
    for u in range(TURN):
        values_ref[count + u] = jnp.zeros((species, SB), F32)
        cells_out[count + u] = jnp.full((species, SB), -1, jnp.int32)
        list_ref[LIST + count + u] = 0
    room = cells_out.shape[0]
    depth = DEPTHS[0]
    edges = strip_pack(lat_ref, WIDTHS[0], 0) + strip_pack(lat_ref, WIDTHS[0], 1)
    for row in list(range(depth)) + list(range(rows - depth, rows)):
        edges += load_row(lat_ref, row)
    for i, tile in enumerate(edges):
        values_ref[room + i] = tile


def gather_latent(first, site_cells, lat_rows):
    sources, blocks, lanes = site_cells.shape
    rows, species, cols = lat_rows.shape
    room = sources * blocks + 2 * TURN
    strips = strip_counts(rows)[0]
    f32 = lambda *s: jax.ShapeDtypeStruct(s, F32)
    i32 = lambda *s: jax.ShapeDtypeStruct(s, jnp.int32)
    return pl.pallas_call(
        gather_kernel,
        in_specs=[whole(SMEM), whole(), whole()],
        out_specs=[whole()] * 2 + [whole(SMEM)],
        out_shape=[
            f32(room + 2 * strips + 2 * DEPTHS[0] * (cols // LANES), species, lanes),
            i32(room, species, lanes),
            i32(LIST + room),
        ],
        compiler_params=params(56),
        cost_estimate=cost(16 * room * lanes * species, 8 * room * lanes * species),
        name="gather_latent",
    )(first, site_cells, lat_rows)


def hi_lo(value):
    high = value.astype(BF16)
    low = (value - high.astype(F32)).astype(BF16)
    return high, low


def site_kernel(list_hbm, cells_hbm, values_hbm, sites_hbm,
                g_ref, w_ref, left_ref, right_ref, up_ref, down_ref,
                list_ref, cells_ref, values_ref, sites_ref, lat_ref, in_sem, small_sem):
    rows, species, cols = g_ref.shape
    sources, _, slots = sites_ref.shape
    blocks = slots // SB
    tiles = cols // LANES
    list_copy = pltpu.make_async_copy(list_hbm, list_ref, small_sem.at[0])
    list_copy.start()
    loads = []
    for stage in range(STAGES):
        size = sources // STAGES
        last = stage == STAGES - 1
        spots = pl.ds(stage * size * blocks, size * blocks + (TURN if last else 0))
        for i, (src, dst, part) in enumerate((
            (sites_hbm, sites_ref, pl.ds(stage * size, size)),
            (values_hbm, values_ref, spots),
            (cells_hbm, cells_ref, spots),
        )):
            copy = pltpu.make_async_copy(src.at[part], dst.at[part], in_sem.at[3 * stage + i])
            copy.start()
            loads.append(copy)
    tail = pl.ds(cells_ref.shape[0], lat_ref.shape[0])
    lat_copy = pltpu.make_async_copy(values_hbm.at[tail], lat_ref, small_sem.at[1])
    lat_copy.start()
    g_ref[...] = jnp.zeros_like(g_ref)
    w_ref[...] = jnp.zeros_like(w_ref)
    lane_of = lax.broadcasted_iota(jnp.int32, (LANES, SB), 0).astype(jnp.int16)
    one = jnp.ones((LANES, SB), BF16)
    zero = jnp.zeros((LANES, SB), BF16)
    zero16 = jnp.zeros((2 * species, SB), BF16)

    def place(at):
        block = list_ref[LIST + at] // rows
        source = block // blocks
        spot = pl.ds(pl.multiple_of((block % blocks) * SB, SB), SB)
        cell = jnp.concatenate([cells_ref[at]] * 2, axis=0)
        low = (cell & (LANES - 1)).astype(jnp.int16)
        high = jnp.where(cell < 0, -1, (cell // LANES) & (tiles - 1)).astype(jnp.int16)
        eta = values_ref[at] + sites_ref[source, :species, spot]
        ratio = sites_ref[source, species:, spot]
        e = jnp.exp(-eta)
        psi = 1.0 / (1.0 + e)
        ep = e * psi
        weight = ep * psi
        gradient = ep * (1.0 - ratio) / (1.0 + e * ratio)
        both_hi, both_lo = hi_lo(jnp.concatenate([weight, gradient], axis=0))
        hot = jnp.where(lane_of == jnp.concatenate([low] * (LANES // low.shape[0]), axis=0), one, zero)
        placed_hi = []
        placed_lo = []
        for t in range(tiles):
            here = high == t
            placed_hi.append(jnp.where(here, both_hi, zero16))
            placed_lo.append(jnp.where(here, both_lo, zero16))
        left = jnp.concatenate(
            [jnp.concatenate(placed_hi, axis=0), jnp.concatenate(placed_lo, axis=0)], axis=1
        )
        right = jnp.concatenate([hot, hot], axis=1)
        return lax.dot_general(left, right, (((1,), (1,)), ((), ())), preferred_element_type=F32)

    def turn(i, carry):
        at = [i * TURN + u for u in range(TURN)]
        for spot in at:
            placed = place(spot)
            row = list_ref[LIST + spot] % rows
            for t in range(tiles):
                lanes = pl.ds(t * LANES, LANES)
                start = 2 * species * t
                w_ref[row, :, lanes] += placed[start:start + species]
                g_ref[row, :, lanes] += placed[start + species:start + 2 * species]
        return carry

    list_copy.wait()
    for stage in range(STAGES):
        for copy in loads[3 * stage:3 * stage + 3]:
            copy.wait()
        first = list_ref[stage] // TURN
        end = list_ref[stage + 1]
        if stage == STAGES - 1:
            end = end + TURN - 1
        lax.fori_loop(first, end // TURN, turn, 0)

    lat_copy.wait()
    lat_strips = strip_counts(rows)[0]
    for side, ref in ((0, left_ref), (1, right_ref)):
        strips = [lat_ref[side * lat_strips + i] for i in range(lat_strips)]
        strips += strip_pack(g_ref, WIDTHS[1], side) + strip_pack(w_ref, WIDTHS[2], side)
        for i, strip in enumerate(strips):
            ref[i] = strip
    for ref, low_side in ((up_ref, True), (down_ref, False)):
        i = DEPTHS[0] * tiles
        base = 2 * lat_strips + (0 if low_side else i)
        for t in range(i):
            ref[t] = lat_ref[base + t]
        for field, depth in zip((g_ref, w_ref), DEPTHS[1:]):
            for row in range(depth) if low_side else range(rows - depth, rows):
                for tile in load_row(field, row):
                    ref[i] = tile
                    i += 1
        for j in range(i, ref.shape[0]):
            ref[j] = jnp.zeros((species, LANES), F32)


def site_terms(values, cells, block_list, sites, rows, cols):
    species = values.shape[1]
    counts = strip_counts(rows)
    strips = sum(counts)
    edge_tiles = sum(DEPTHS) * (cols // LANES) + 2 * sum(counts)
    shape = lambda *s: jax.ShapeDtypeStruct(s, F32)
    return pl.pallas_call(
        site_kernel,
        in_specs=[in_hbm()] * 4,
        out_specs=[whole()] * 6,
        out_shape=[
            shape(rows, species, cols),
            shape(rows, species, cols),
            shape(strips, species, LANES),
            shape(strips, species, LANES),
            shape(edge_tiles, species, LANES),
            shape(edge_tiles, species, LANES),
        ],
        scratch_shapes=[
            SMEM(block_list.shape, jnp.int32),
            VMEM(cells.shape, jnp.int32),
            VMEM(cells.shape, F32),
            VMEM(sites.shape, F32),
            VMEM((values.shape[0] - cells.shape[0], species, LANES), F32),
            dma(3 * STAGES),
            dma(2),
        ],
        compiler_params=params(48),
        name="site_terms",
    )(block_list, cells, values, sites)


def krylov_kernel(ksq_ref, lat_ref, g_ref, w_ref, right_ref, left_ref, up_ref, down_ref,
                  b_out, h_out, h2_out, part_ref, lx, bx, wx, m_ref):
    rows, species, cols = g_ref.shape
    tiles = cols // LANES
    lane = lax.broadcasted_iota(jnp.int32, (species, LANES), 1)
    ksq = per_species(ksq_ref)
    ksq4 = ksq + 4.0
    scale = 4.0 * math.pi * ksq
    edges = Edges(lane)
    halo = pl.ds(cols, LANES)
    counts = strip_counts(rows)
    exts = (lx, bx, wx)

    def strips(ref, base):
        out = []
        for count in counts:
            out.append([ref[base + i] for i in range(count)])
            base += count
        return out

    right = strips(right_ref, 0)
    left = strips(left_ref, 0)
    for field, ext, depth, width, r, l in zip((lat_ref, g_ref, w_ref), exts, DEPTHS, WIDTHS, right, left):
        ext[depth:rows + depth, :, :cols] = field[...]
        for row in range(rows):
            ext[depth + row, :, halo] = halo_tile(r, l, row, width, lane)
    for ref, above in ((up_ref, True), (down_ref, False)):
        base = sum(DEPTHS) * tiles
        right = strips(ref, base)
        left = strips(ref, base + sum(counts))
        i = 0
        for ext, depth, width, r, l in zip(exts, DEPTHS, WIDTHS, right, left):
            for row in range(depth):
                to = row if above else rows + depth + row
                came = rows - depth + row if above else row
                for t in range(tiles):
                    ext[to, :, t * LANES:(t + 1) * LANES] = ref[i]
                    i += 1
                ext[to, :, halo] = halo_tile(r, l, came, width, lane)

    def factor(src, src_pad, row, count=None):
        return factor_row(src, row + src_pad, ksq4, lane, count)

    def run(first, last, pad, row_tiles, dst):
        edges.pass_rows(first + pad, last + pad, pad, rows + pad, lambda r: row_tiles(r - pad), dst)

    run(-5, rows + 5, 5, lambda r: factor(lx, 6, r), m_ref)

    def right_side(r):
        return [g - scale * f for g, f in zip(load_row(bx, r + 4), factor(m_ref, 5, r))]

    run(-4, rows + 4, 4, right_side, bx)
    run(-3, rows + 3, 5, lambda r: factor(bx, 4, r), m_ref)

    def image(r):
        b = load_row(bx, r + 4)
        w = load_row(wx, r + 2)
        return [scale * f + x * y for f, x, y in zip(factor(m_ref, 5, r), w, b)]

    run(-2, rows + 2, 6, image, lx)
    run(-1, rows + 1, 5, lambda r: factor(lx, 6, r), m_ref)

    zero = jnp.zeros((species, LANES), F32)
    group = 8

    def sum_turn(i, sums):
        bb, bh, hh, hh2 = sums
        for u in range(group):
            row = i * group + u
            for t, f in enumerate(factor(m_ref, 5, row, tiles)):
                lanes = pl.ds(t * LANES, LANES)
                b = bx[row + 4, :, lanes]
                h = lx[row + 6, :, lanes]
                h2 = scale * f + wx[row + 2, :, lanes] * h
                b_out[row, :, lanes] = b
                h_out[row, :, lanes] = h
                h2_out[row, :, lanes] = h2
                bb = bb + b * b
                bh = bh + b * h
                hh = hh + h * h
                hh2 = hh2 + h * h2
        return bb, bh, hh, hh2

    sums = lax.fori_loop(0, rows // group, sum_turn, (zero, zero, zero, zero))
    lane_row = lax.broadcasted_iota(jnp.int32, part_ref.shape, 1)
    part = jnp.zeros(part_ref.shape, F32)
    for i, total in enumerate(sums):
        narrow = jnp.sum(total, axis=0, keepdims=True)
        narrow = jnp.sum(narrow, axis=1, keepdims=True)
        part = jnp.where(lane_row == i, narrow, part)
    part_ref[...] = part


def krylov(ksq, lat_rows, g, w, right, left, from_up, from_down, devices):
    rows, species, cols = g.shape
    ext = lambda pad: (rows + 2 * pad, species, cols + LANES)
    shape = lambda *s: jax.ShapeDtypeStruct(s, F32)
    field = shape(rows, species, cols)
    return pl.pallas_call(
        krylov_kernel,
        in_specs=[whole(SMEM)] + [whole()] * 7,
        out_specs=[whole()] * 4,
        out_shape=[field, field, field, shape(devices, LANES)],
        scratch_shapes=[VMEM(ext(pad), F32) for pad in (6, 4, 2, 5)],
        compiler_params=params(20),
        name="krylov",
    )(ksq, lat_rows, g, w, right, left, from_up, from_down)


def finish_kernel(parts_ref, b_ref, h_ref, h2_ref, step_ref, residual_ref):
    total = jnp.sum(parts_ref[...], axis=0, keepdims=True)
    lane = lax.broadcasted_iota(jnp.int32, total.shape, 1)

    def pick(i):
        return jnp.sum(jnp.where(lane == i, total, 0.0), axis=1, keepdims=True)

    bb, bh, hh, hh2 = (pick(i) for i in range(4))
    alpha = bb / bh
    rr = bb - 2.0 * alpha * bh + alpha * alpha * hh
    beta = rr / bb
    grown = 1.0 + beta
    curve = grown * grown * bh - 2.0 * grown * alpha * hh + alpha * alpha * hh2
    later = rr / curve
    c0 = (alpha + later * grown)[None]
    c1 = (later * alpha)[None]
    b = b_ref[...]
    h = h_ref[...]
    step_ref[...] = jnp.swapaxes(c0 * b - c1 * h, 0, 1)
    residual_ref[...] = jnp.swapaxes(b - c0 * h + c1 * h2_ref[...], 0, 1)


def finish(parts, b, h, h2):
    rows, species, cols = b.shape
    group = 32
    field = pl.BlockSpec((group, species, cols), lambda i: (i, 0, 0))
    out = pl.BlockSpec((species, group, cols), lambda i: (0, i, 0))
    shape = jax.ShapeDtypeStruct((species, rows, cols), F32)
    return pl.pallas_call(
        finish_kernel,
        grid=(rows // group,),
        in_specs=[pl.BlockSpec(parts.shape, lambda i: (0, 0)), field, field, field],
        out_specs=[out, out],
        out_shape=[shape, shape],
        compiler_params=params(24),
        name="finish",
    )(parts, b, h, h2)


def neighbour_pairs(count):
    forward = [(i, i + 1) for i in range(count - 1)]
    backward = [(target, source) for source, target in forward]
    return forward, backward


def per_device(latent, site_offset, site_counts, site_cells, detect_prob, kappa_sq):
    species, rows, cols = latent.shape
    n_gr, n_gc = lax.axis_size("gr"), lax.axis_size("gc")
    down_pairs, up_pairs = neighbour_pairs(n_gr)
    right_pairs, left_pairs = neighbour_pairs(n_gc)
    sites = lax.all_to_all(
        pack_sites(site_offset, site_counts, detect_prob), MESH, split_axis=0, concat_axis=0, tiled=True
    )
    lat_rows = jnp.transpose(latent, (1, 0, 2))
    first = site_cells[:, ::SB].reshape(-1)
    site_cells = site_cells.reshape(site_cells.shape[0], -1, SB)
    blocks = gather_latent(first, site_cells, lat_rows)

    g, w, to_left, to_right, to_up, to_down = site_terms(*blocks, sites, rows, cols)
    from_left = lax.ppermute(to_right, "gc", right_pairs)
    from_right = lax.ppermute(to_left, "gc", left_pairs)
    strips = jnp.concatenate([from_right, from_left], axis=0)
    spot = (to_up.shape[0] - strips.shape[0], 0, 0)
    to_up = lax.dynamic_update_slice(to_up, strips, spot)
    to_down = lax.dynamic_update_slice(to_down, strips, spot)
    from_up = lax.ppermute(to_down, "gr", down_pairs)
    from_down = lax.ppermute(to_up, "gr", up_pairs)

    b, h, h2, part = krylov(kappa_sq, lat_rows, g, w, from_right, from_left, from_up, from_down, n_gr * n_gc)
    parts = lax.all_to_all(part, MESH, split_axis=0, concat_axis=0, tiled=True)
    return finish(parts, b, h, h2)


def solution(mesh):
    in_specs = (
        P(None, "gr", "gc"),
        P(None, ("gr", "gc"), None),
        P(None, ("gr", "gc"), None),
        P(("gr", "gc"), None),
        P(),
        P(),
    )
    out_specs = (P(None, "gr", "gc"), P(None, "gr", "gc"))
    return jax.shard_map(
        per_device, mesh=mesh, in_specs=in_specs, out_specs=out_specs, check_vma=False
    )
```

```python
import functools
import math

import jax
import jax.numpy as jnp
from jax import lax
from jax.experimental import pallas as pl
from jax.experimental.pallas import tpu as pltpu
from jax.sharding import PartitionSpec as P

SB = 128
VISITS = 4
LANES = 128
MESH = ("gr", "gc")
VMEM = pltpu.VMEM
SMEM = pltpu.SMEM
F32 = jnp.float32
BF16 = jnp.bfloat16


def whole(space=VMEM):
    return pl.BlockSpec(memory_space=space)


def params(mib):
    return pltpu.CompilerParams(vmem_limit_bytes=mib * 1024 * 1024)


def in_hbm():
    return pl.BlockSpec(memory_space=pltpu.HBM)


def dma(count):
    return pltpu.SemaphoreType.DMA((count,))


def cost(flops, moved):
    return pl.CostEstimate(flops=flops, bytes_accessed=moved, transcendentals=0)


def per_species(ref):
    species = ref.shape[0]
    row = lax.broadcasted_iota(jnp.int32, (species, LANES), 0)
    out = jnp.zeros((species, LANES), F32)
    for k in range(species):
        out = jnp.where(row == k, ref[k], out)
    return out


def pack_kernel(prob_ref, offset_hbm, counts_hbm, out_hbm, offset, counts, out, in_sem, out_sem):
    species, owners, slots = offset.shape
    pieces = in_sem.shape[0] // 2
    size = owners // pieces
    loads = []
    for p in range(pieces):
        part = pl.ds(p * size, size)
        for i, (src, dst) in enumerate(((offset_hbm, offset), (counts_hbm, counts))):
            copy = pltpu.make_async_copy(src.at[:, part], dst.at[:, part], in_sem.at[2 * p + i])
            copy.start()
            loads.append(copy)
    prob = per_species(prob_ref)
    square = (1.0 - prob) * (1.0 - prob)
    q = (1.0 / (square * square))[None]
    group = 8
    stores = []
    for p in range(pieces):
        loads[2 * p].wait()
        loads[2 * p + 1].wait()

        def turn(i, carry):
            rows = pl.ds(pl.multiple_of(p * size + i * group, group), group)
            for t in range(slots // LANES):
                lanes = pl.ds(t * LANES, LANES)
                offsets = jnp.swapaxes(offset[:, rows, lanes], 0, 1)
                found = jnp.swapaxes(counts[:, rows, lanes], 0, 1)
                out[rows, :species, lanes] = offsets
                out[rows, species:, lanes] = jnp.where(found > 0, jnp.zeros_like(offsets), q)
            return carry

        lax.fori_loop(0, size // group, turn, 0)
        part = pl.ds(p * size, size)
        copy = pltpu.make_async_copy(out.at[part], out_hbm.at[part], out_sem.at[p])
        copy.start()
        stores.append(copy)
    for copy in stores:
        copy.wait()


def pack_sites(site_offset, site_counts, detect_prob):
    species, owners, slots = site_offset.shape
    pieces = 8
    return pl.pallas_call(
        pack_kernel,
        in_specs=[whole(SMEM), in_hbm(), in_hbm()],
        out_specs=in_hbm(),
        out_shape=jax.ShapeDtypeStruct((owners, 2 * species, slots), F32),
        scratch_shapes=[
            VMEM(site_offset.shape, F32),
            VMEM(site_offset.shape, jnp.int32),
            VMEM((owners, 2 * species, slots), F32),
            dma(2 * pieces),
            dma(pieces),
        ],
        compiler_params=params(56),
        name="pack_sites",
    )(detect_prob, site_offset, site_counts)


def load_row(ref, row):
    return [ref[row, :, t * LANES:(t + 1) * LANES] for t in range(ref.shape[2] // LANES)]


def store_row(ref, row, tiles):
    for t, tile in enumerate(tiles):
        ref[row, :, t * LANES:(t + 1) * LANES] = tile


def factor_row(ref, row, ksq4, lane, count=None):
    center = load_row(ref, row)
    above = load_row(ref, row - 1)
    below = load_row(ref, row + 1)
    total = len(center)
    right = [pltpu.roll(tile, 1, 1) for tile in center]
    left = [pltpu.roll(tile, LANES - 1, 1) for tile in center]
    out = []
    for t in range(count or total):
        from_left = jnp.where(lane == 0, right[t - 1], right[t])
        from_right = jnp.where(lane == LANES - 1, left[(t + 1) % total], left[t])
        out.append(ksq4 * center[t] - ((above[t] + below[t]) + (from_left + from_right)))
    return out


def each_row(first, last, body, chunk=32):
    turns = (last - first) // chunk

    def turn(i, carry):
        for u in range(chunk):
            body(first + i * chunk + u)
        return carry

    lax.fori_loop(0, turns, turn, 0)
    for row in range(first + turns * chunk, last):
        body(row)


class Edges:
    def __init__(self, lane):
        gr, gc = lax.axis_index("gr"), lax.axis_index("gc")
        self.up, self.down, left, right = (
            jnp.where(there, jnp.float32(1.0), jnp.float32(0.0))
            for there in (
                gr > 0,
                gr < lax.axis_size("gr") - 1,
                gc > 0,
                gc < lax.axis_size("gc") - 1,
            )
        )
        self.halo = jnp.where(lane < LANES // 2, right, left)

    def pass_rows(self, first, last, low, high, row_tiles, dst_ref):
        def put(row, scale):
            tiles = row_tiles(row)
            tiles[-1] = tiles[-1] * self.halo
            if scale is not None:
                tiles = [tile * scale for tile in tiles]
            store_row(dst_ref, row, tiles)

        for row in range(first, low):
            put(row, self.up)
        each_row(low, high, lambda row: put(row, None))
        for row in range(high, last):
            put(row, self.down)


def strip_pack(field_ref, width, side):
    rows, species, cols = field_ref.shape
    per_tile = LANES // width
    lane = lax.broadcasted_iota(jnp.int32, (species, LANES), 1) // width
    tiles = []
    for tile in range(rows // per_tile):
        packed = jnp.zeros((species, LANES), F32)
        for p in range(per_tile):
            row = tile * per_tile + p
            if side == 0:
                part = field_ref[row, :, :LANES]
                shift = (p * width) % LANES
            else:
                part = field_ref[row, :, cols - LANES:]
                shift = (p * width + width) % LANES
            if shift:
                part = pltpu.roll(part, shift, 1)
            packed = jnp.where(lane == p, part, packed)
        tiles.append(packed)
    return tiles


def halo_tile(right_tiles, left_tiles, row, width, lane):
    per_tile = LANES // width
    tile, p = row // per_tile, row % per_tile
    shift = (LANES - p * width) % LANES
    from_right = pltpu.roll(right_tiles[tile], shift, 1) if shift else right_tiles[tile]
    shift = (LANES - p * width - width) % LANES
    from_left = pltpu.roll(left_tiles[tile], shift, 1) if shift else left_tiles[tile]
    return jnp.where(lane < width, from_right, jnp.where(lane >= LANES - width, from_left, 0.0))


WIDTHS = (8, 4, 2)
DEPTHS = (6, 4, 2)
TURN = 32
STAGES = 4
LIST = 8


def strip_counts(rows):
    return [rows * width // LANES for width in WIDTHS]


def gather_kernel(first_ref, cells_ref, lat_ref, values_ref, cells_out, list_ref):
    sources, blocks = cells_ref.shape[:2]
    rows, species, cols = lat_ref.shape
    tiles = cols // LANES
    total = sources * blocks
    per_stage = sources // STAGES

    def step(source, spot):
        for j in range(blocks):
            cell = cells_ref[source, j:j + 1, :]
            first = first_ref[source * blocks + j]
            row = jnp.maximum(first, 0) // cols
            live = first >= 0
            at = jnp.where(live, spot, total + TURN)
            wide = jnp.broadcast_to(cell, (species, SB))
            low = wide & (LANES - 1)
            high = (wide // LANES) & (tiles - 1)
            value = jnp.zeros((species, SB), F32)
            for t in range(tiles):
                part = lat_ref[row, :, t * LANES:(t + 1) * LANES]
                picked = jnp.take_along_axis(part, low, axis=1)
                value = jnp.where(high == t, picked, value)
            values_ref[at] = value
            cells_out[at] = wide
            list_ref[LIST + at] = (source * blocks + j) * rows + row
            spot = spot + live.astype(jnp.int32)
        return spot

    count = jnp.int32(0)
    for stage in range(STAGES):
        list_ref[stage] = count
        count = lax.fori_loop(stage * per_stage, (stage + 1) * per_stage, step, count)
    list_ref[STAGES] = count
    for u in range(TURN):
        values_ref[count + u] = jnp.zeros((species, SB), F32)
        cells_out[count + u] = jnp.full((species, SB), -1, jnp.int32)
        list_ref[LIST + count + u] = 0
    room = cells_out.shape[0]
    depth = DEPTHS[0]
    edges = strip_pack(lat_ref, WIDTHS[0], 0) + strip_pack(lat_ref, WIDTHS[0], 1)
    for row in list(range(depth)) + list(range(rows - depth, rows)):
        edges += load_row(lat_ref, row)
    for i, tile in enumerate(edges):
        values_ref[room + i] = tile


def gather_latent(first, site_cells, lat_rows):
    sources, blocks, lanes = site_cells.shape
    rows, species, cols = lat_rows.shape
    room = sources * blocks + 2 * TURN
    strips = strip_counts(rows)[0]
    f32 = lambda *s: jax.ShapeDtypeStruct(s, F32)
    i32 = lambda *s: jax.ShapeDtypeStruct(s, jnp.int32)
    return pl.pallas_call(
        gather_kernel,
        in_specs=[whole(SMEM), whole(), whole()],
        out_specs=[whole()] * 2 + [whole(SMEM)],
        out_shape=[
            f32(room + 2 * strips + 2 * DEPTHS[0] * (cols // LANES), species, lanes),
            i32(room, species, lanes),
            i32(LIST + room),
        ],
        compiler_params=params(56),
        cost_estimate=cost(16 * room * lanes * species, 8 * room * lanes * species),
        name="gather_latent",
    )(first, site_cells, lat_rows)


def hi_lo(value):
    high = value.astype(BF16)
    low = (value - high.astype(F32)).astype(BF16)
    return high, low


def site_kernel(list_hbm, cells_hbm, values_hbm, sites_hbm,
                g_ref, w_ref, left_ref, right_ref, up_ref, down_ref,
                list_ref, cells_ref, values_ref, sites_ref, lat_ref, in_sem, small_sem):
    rows, species, cols = g_ref.shape
    sources, _, slots = sites_ref.shape
    blocks = slots // SB
    tiles = cols // LANES
    list_copy = pltpu.make_async_copy(list_hbm, list_ref, small_sem.at[0])
    list_copy.start()
    loads = []
    for stage in range(STAGES):
        size = sources // STAGES
        last = stage == STAGES - 1
        spots = pl.ds(stage * size * blocks, size * blocks + (TURN if last else 0))
        for i, (src, dst, part) in enumerate((
            (sites_hbm, sites_ref, pl.ds(stage * size, size)),
            (values_hbm, values_ref, spots),
            (cells_hbm, cells_ref, spots),
        )):
            copy = pltpu.make_async_copy(src.at[part], dst.at[part], in_sem.at[3 * stage + i])
            copy.start()
            loads.append(copy)
    tail = pl.ds(cells_ref.shape[0], lat_ref.shape[0])
    lat_copy = pltpu.make_async_copy(values_hbm.at[tail], lat_ref, small_sem.at[1])
    lat_copy.start()
    g_ref[...] = jnp.zeros_like(g_ref)
    w_ref[...] = jnp.zeros_like(w_ref)
    lane_of = lax.broadcasted_iota(jnp.int32, (LANES, SB), 0).astype(jnp.int16)
    one = jnp.ones((LANES, SB), BF16)
    zero = jnp.zeros((LANES, SB), BF16)
    zero16 = jnp.zeros((2 * species, SB), BF16)

    def place(at):
        block = list_ref[LIST + at] // rows
        source = block // blocks
        spot = pl.ds(pl.multiple_of((block % blocks) * SB, SB), SB)
        cell = jnp.concatenate([cells_ref[at]] * 2, axis=0)
        low = (cell & (LANES - 1)).astype(jnp.int16)
        high = jnp.where(cell < 0, -1, (cell // LANES) & (tiles - 1)).astype(jnp.int16)
        eta = values_ref[at] + sites_ref[source, :species, spot]
        ratio = sites_ref[source, species:, spot]
        e = jnp.exp(-eta)
        psi = 1.0 / (1.0 + e)
        ep = e * psi
        weight = ep * psi
        gradient = ep * (1.0 - ratio) / (1.0 + e * ratio)
        both_hi, both_lo = hi_lo(jnp.concatenate([weight, gradient], axis=0))
        hot = jnp.where(lane_of == jnp.concatenate([low] * (LANES // low.shape[0]), axis=0), one, zero)
        placed_hi = []
        placed_lo = []
        for t in range(tiles):
            here = high == t
            placed_hi.append(jnp.where(here, both_hi, zero16))
            placed_lo.append(jnp.where(here, both_lo, zero16))
        left = jnp.concatenate(
            [jnp.concatenate(placed_hi, axis=0), jnp.concatenate(placed_lo, axis=0)], axis=1
        )
        right = jnp.concatenate([hot, hot], axis=1)
        return lax.dot_general(left, right, (((1,), (1,)), ((), ())), preferred_element_type=F32)

    def turn(i, carry):
        at = [i * TURN + u for u in range(TURN)]
        for spot in at:
            placed = place(spot)
            row = list_ref[LIST + spot] % rows
            for t in range(tiles):
                lanes = pl.ds(t * LANES, LANES)
                start = 2 * species * t
                w_ref[row, :, lanes] += placed[start:start + species]
                g_ref[row, :, lanes] += placed[start + species:start + 2 * species]
        return carry

    list_copy.wait()
    for stage in range(STAGES):
        for copy in loads[3 * stage:3 * stage + 3]:
            copy.wait()
        first = list_ref[stage] // TURN
        end = list_ref[stage + 1]
        if stage == STAGES - 1:
            end = end + TURN - 1
        lax.fori_loop(first, end // TURN, turn, 0)

    lat_copy.wait()
    lat_strips = strip_counts(rows)[0]
    for side, ref in ((0, left_ref), (1, right_ref)):
        strips = [lat_ref[side * lat_strips + i] for i in range(lat_strips)]
        strips += strip_pack(g_ref, WIDTHS[1], side) + strip_pack(w_ref, WIDTHS[2], side)
        for i, strip in enumerate(strips):
            ref[i] = strip
    for ref, low_side in ((up_ref, True), (down_ref, False)):
        i = DEPTHS[0] * tiles
        base = 2 * lat_strips + (0 if low_side else i)
        for t in range(i):
            ref[t] = lat_ref[base + t]
        for field, depth in zip((g_ref, w_ref), DEPTHS[1:]):
            for row in range(depth) if low_side else range(rows - depth, rows):
                for tile in load_row(field, row):
                    ref[i] = tile
                    i += 1
        for j in range(i, ref.shape[0]):
            ref[j] = jnp.zeros((species, LANES), F32)


def site_terms(values, cells, block_list, sites, rows, cols):
    species = values.shape[1]
    counts = strip_counts(rows)
    strips = sum(counts)
    edge_tiles = sum(DEPTHS) * (cols // LANES) + 2 * sum(counts)
    shape = lambda *s: jax.ShapeDtypeStruct(s, F32)
    return pl.pallas_call(
        site_kernel,
        in_specs=[in_hbm()] * 4,
        out_specs=[whole()] * 6,
        out_shape=[
            shape(rows, species, cols),
            shape(rows, species, cols),
            shape(strips, species, LANES),
            shape(strips, species, LANES),
            shape(edge_tiles, species, LANES),
            shape(edge_tiles, species, LANES),
        ],
        scratch_shapes=[
            SMEM(block_list.shape, jnp.int32),
            VMEM(cells.shape, jnp.int32),
            VMEM(cells.shape, F32),
            VMEM(sites.shape, F32),
            VMEM((values.shape[0] - cells.shape[0], species, LANES), F32),
            dma(3 * STAGES),
            dma(2),
        ],
        compiler_params=params(48),
        name="site_terms",
    )(block_list, cells, values, sites)


RIM = 6
PADS = (6, 4, 2)
MID_PAD = 5


class Krylov:
    def __init__(self, ksq_ref, scratch):
        self.lx, self.bx, self.wx, self.mid = scratch
        species = ksq_ref.shape[0]
        self.lane = lax.broadcasted_iota(jnp.int32, (species, LANES), 1)
        ksq = per_species(ksq_ref)
        self.ksq4 = ksq + 4.0
        self.scale = 4.0 * math.pi * ksq
        self.edges = Edges(self.lane)
        self.zero = jnp.zeros((species, LANES), F32)

    def factor(self, src, pad, row, count=None):
        return factor_row(src, row + pad, self.ksq4, self.lane, count)

    def passes(self, first, last, low, high):
        lx, bx, wx, mid = self.lx, self.bx, self.wx, self.mid
        scale = self.scale

        def run(reach, pad, row_tiles, dst):
            f, l = first - reach, last + reach
            self.edges.pass_rows(
                f + pad, l + pad, max(f, low) + pad, min(l, high) + pad, lambda r: row_tiles(r - pad), dst
            )

        def right_side(r):
            return [g - scale * f for g, f in zip(load_row(bx, r + 4), self.factor(mid, MID_PAD, r))]

        def image(r):
            both = zip(self.factor(mid, MID_PAD, r), load_row(wx, r + 2), load_row(bx, r + 4))
            return [scale * f + w * b for f, w, b in both]

        run(5, MID_PAD, lambda r: self.factor(lx, 6, r), mid)
        run(4, 4, right_side, bx)
        run(3, MID_PAD, lambda r: self.factor(bx, 4, r), mid)
        run(2, 6, image, lx)
        run(1, MID_PAD, lambda r: self.factor(lx, 6, r), mid)

    def last(self, row, tiles, outs, to, sums):
        bb, bh, hh, hh2 = sums
        for t, f in enumerate(self.factor(self.mid, MID_PAD, row, tiles)):
            lanes = pl.ds(t * LANES, LANES)
            b = self.bx[row + 4, :, lanes]
            h = self.lx[row + 6, :, lanes]
            h2 = self.scale * f + self.wx[row + 2, :, lanes] * h
            for ref, value in zip(outs, (b, h, h2)):
                ref[to, :, lanes] = value
            bb = bb + b * b
            bh = bh + b * h
            hh = hh + h * h
            hh2 = hh2 + h * h2
        return bb, bh, hh, hh2


def strips_of(ref, base, rows):
    out = []
    for count in strip_counts(rows):
        out.append([ref[base + i] for i in range(count)])
        base += count
    return out


def inner_kernel(ksq_ref, lat_ref, g_ref, w_ref, right_ref, left_ref, b_out, h_out, h2_out, sums_ref, *scratch):
    rows, species, cols = g_ref.shape
    krylov = Krylov(ksq_ref, scratch)
    right = strips_of(right_ref, 0, rows)
    left = strips_of(left_ref, 0, rows)
    halo = pl.ds(cols, LANES)
    for field, ext, pad, width, r, l in zip((lat_ref, g_ref, w_ref), scratch, PADS, WIDTHS, right, left):
        ext[pad:rows + pad, :, :cols] = field[...]
        for row in range(rows):
            ext[pad + row, :, halo] = halo_tile(r, l, row, width, krylov.lane)
    krylov.passes(RIM, rows - RIM, 0, rows)
    wanted = rows - 2 * RIM
    group = max(d for d in range(1, 17) if wanted % d == 0)

    def turn(i, sums):
        for u in range(group):
            row = RIM + i * group + u
            sums = krylov.last(row, cols // LANES, (b_out, h_out, h2_out), row, sums)
        return sums

    sums = lax.fori_loop(0, wanted // group, turn, (krylov.zero,) * 4)
    for i, total in enumerate(sums):
        sums_ref[i] = total


def scratch_of(rows, species, cols):
    return [VMEM((rows + 2 * pad, species, cols + LANES), F32) for pad in PADS + (MID_PAD,)]


def inner(ksq, lat_rows, g, w, right, left):
    rows, species, cols = g.shape
    shape = lambda *s: jax.ShapeDtypeStruct(s, F32)
    field = shape(rows, species, cols)
    return pl.pallas_call(
        inner_kernel,
        in_specs=[whole(SMEM)] + [whole()] * 5,
        out_specs=[whole()] * 4,
        out_shape=[field, field, field, shape(4, species, LANES)],
        scratch_shapes=scratch_of(rows, species, cols),
        compiler_params=params(20),
        cost_estimate=cost(80 * rows * species * cols, 64 * rows * species * cols),
        name="krylov_inner",
    )(ksq, lat_rows, g, w, right, left)


def rim_kernel(ksq_ref, lat_ref, g_ref, w_ref, right_ref, left_ref, up_ref, down_ref, sums_ref,
               b_out, h_out, h2_out, part_ref, *scratch):
    rows, species, cols = g_ref.shape
    tiles = cols // LANES
    krylov = Krylov(ksq_ref, scratch)
    lane = krylov.lane
    fields = (lat_ref, g_ref, w_ref)
    halo = pl.ds(cols, LANES)
    own_right = strips_of(right_ref, 0, rows)
    own_left = strips_of(left_ref, 0, rows)
    base = sum(DEPTHS) * tiles
    sums = tuple(sums_ref[i] for i in range(4))
    for ref, above in ((up_ref, True), (down_ref, False)):
        start = 0 if above else rows - RIM
        came_right = strips_of(ref, base, rows)
        came_left = strips_of(ref, base + sum(strip_counts(rows)), rows)
        i = 0
        for n, (field, ext, pad, width) in enumerate(zip(fields, scratch, PADS, WIDTHS)):
            for local in range(-pad, RIM + pad):
                own = start + local
                to = local + pad
                if 0 <= own < rows:
                    store_row(ext, to, load_row(field, own))
                    ext[to, :, halo] = halo_tile(own_right[n], own_left[n], own, width, lane)
                else:
                    for t in range(tiles):
                        ext[to, :, t * LANES:(t + 1) * LANES] = ref[i]
                        i += 1
                    came = own % rows
                    ext[to, :, halo] = halo_tile(came_right[n], came_left[n], came, width, lane)
        if above:
            krylov.passes(0, RIM, 0, RIM + 6)
        else:
            krylov.passes(0, RIM, -6, RIM)
        for row in range(RIM):
            to = row if above else RIM + row
            sums = krylov.last(row, tiles, (b_out, h_out, h2_out), to, sums)
    lane_row = lax.broadcasted_iota(jnp.int32, part_ref.shape, 1)
    part = jnp.zeros(part_ref.shape, F32)
    for i, total in enumerate(sums):
        narrow = jnp.sum(total, axis=0, keepdims=True)
        narrow = jnp.sum(narrow, axis=1, keepdims=True)
        part = jnp.where(lane_row == i, narrow, part)
    part_ref[...] = part


def rim(ksq, lat_rows, g, w, right, left, from_up, from_down, sums, devices):
    rows, species, cols = g.shape
    shape = lambda *s: jax.ShapeDtypeStruct(s, F32)
    field = shape(2 * RIM, species, cols)
    return pl.pallas_call(
        rim_kernel,
        in_specs=[whole(SMEM)] + [whole()] * 8,
        out_specs=[whole()] * 4,
        out_shape=[field, field, field, shape(devices, LANES)],
        scratch_shapes=scratch_of(RIM, species, cols),
        compiler_params=params(16),
        name="krylov_rim",
    )(ksq, lat_rows, g, w, right, left, from_up, from_down, sums)


def finish_kernel(parts_ref, b_ref, h_ref, h2_ref, b_rim, h_rim, h2_rim, step_ref, residual_ref):
    total = jnp.sum(parts_ref[...], axis=0, keepdims=True)
    lane = lax.broadcasted_iota(jnp.int32, total.shape, 1)

    def pick(i):
        return jnp.sum(jnp.where(lane == i, total, 0.0), axis=1, keepdims=True)

    bb, bh, hh, hh2 = (pick(i) for i in range(4))
    alpha = bb / bh
    rr = bb - 2.0 * alpha * bh + alpha * alpha * hh
    beta = rr / bb
    grown = 1.0 + beta
    curve = grown * grown * bh - 2.0 * grown * alpha * hh + alpha * alpha * hh2
    later = rr / curve
    c0 = (alpha + later * grown)[None]
    c1 = (later * alpha)[None]

    def put(first, b, h, h2):
        spot = pl.ds(first, b.shape[0])
        step_ref[:, spot, :] = jnp.swapaxes(c0 * b - c1 * h, 0, 1)
        residual_ref[:, spot, :] = jnp.swapaxes(b - c0 * h + c1 * h2, 0, 1)

    group = b_ref.shape[0]
    put(0, b_ref[...], h_ref[...], h2_ref[...])
    refs = ((b_ref, b_rim), (h_ref, h_rim), (h2_ref, h2_rim))

    @pl.when(pl.program_id(0) == 0)
    def _():
        put(0, *(jnp.concatenate([edge[:RIM], ref[RIM:8]], axis=0) for ref, edge in refs))

    @pl.when(pl.program_id(0) == pl.num_programs(0) - 1)
    def _():
        put(group - 8, *(jnp.concatenate([ref[group - 8:group - RIM], edge[RIM:]], axis=0) for ref, edge in refs))


def finish(parts, fields, rims):
    rows, species, cols = fields[0].shape
    group = rows // 2
    field = pl.BlockSpec((group, species, cols), lambda i: (i, 0, 0))
    edge = pl.BlockSpec((2 * RIM, species, cols), lambda i: (0, 0, 0))
    out = pl.BlockSpec((species, group, cols), lambda i: (0, i, 0))
    shape = jax.ShapeDtypeStruct((species, rows, cols), F32)
    return pl.pallas_call(
        finish_kernel,
        grid=(rows // group,),
        in_specs=[pl.BlockSpec(parts.shape, lambda i: (0, 0))] + [field] * 3 + [edge] * 3,
        out_specs=[out, out],
        out_shape=[shape, shape],
        compiler_params=params(28),
        name="finish",
    )(parts, *fields, *rims)


def neighbour_pairs(count):
    forward = [(i, i + 1) for i in range(count - 1)]
    backward = [(target, source) for source, target in forward]
    return forward, backward


def per_device(latent, site_offset, site_counts, site_cells, detect_prob, kappa_sq):
    species, rows, cols = latent.shape
    n_gr, n_gc = lax.axis_size("gr"), lax.axis_size("gc")
    down_pairs, up_pairs = neighbour_pairs(n_gr)
    right_pairs, left_pairs = neighbour_pairs(n_gc)
    sites = lax.all_to_all(
        pack_sites(site_offset, site_counts, detect_prob), MESH, split_axis=0, concat_axis=0, tiled=True
    )
    lat_rows = jnp.transpose(latent, (1, 0, 2))
    first = site_cells[:, ::SB].reshape(-1)
    site_cells = site_cells.reshape(site_cells.shape[0], -1, SB)
    blocks = gather_latent(first, site_cells, lat_rows)

    g, w, to_left, to_right, to_up, to_down = site_terms(*blocks, sites, rows, cols)
    from_left = lax.ppermute(to_right, "gc", right_pairs)
    from_right = lax.ppermute(to_left, "gc", left_pairs)
    strips = jnp.concatenate([from_right, from_left], axis=0)
    spot = (to_up.shape[0] - strips.shape[0], 0, 0)
    to_up = lax.dynamic_update_slice(to_up, strips, spot)
    to_down = lax.dynamic_update_slice(to_down, strips, spot)
    from_up = lax.ppermute(to_down, "gr", down_pairs)
    from_down = lax.ppermute(to_up, "gr", up_pairs)

    near = (kappa_sq, lat_rows, g, w, from_right, from_left)
    *fields, sums = inner(*near)
    *rims, part = rim(*near, from_up, from_down, sums, n_gr * n_gc)
    parts = lax.all_to_all(part, MESH, split_axis=0, concat_axis=0, tiled=True)
    return finish(parts, fields, rims)


def solution(mesh):
    in_specs = (
        P(None, "gr", "gc"),
        P(None, ("gr", "gc"), None),
        P(None, ("gr", "gc"), None),
        P(("gr", "gc"), None),
        P(),
        P(),
    )
    out_specs = (P(None, "gr", "gc"), P(None, "gr", "gc"))
    return jax.shard_map(
        per_device, mesh=mesh, in_specs=in_specs, out_specs=out_specs, check_vma=False
    )
```

```python
import functools
import math

import jax
import jax.numpy as jnp
from jax import lax
from jax.experimental import pallas as pl
from jax.experimental.pallas import tpu as pltpu
from jax.sharding import PartitionSpec as P

SB = 128
VISITS = 4
LANES = 128
MESH = ("gr", "gc")
VMEM = pltpu.VMEM
SMEM = pltpu.SMEM
F32 = jnp.float32
BF16 = jnp.bfloat16


def whole(space=VMEM):
    return pl.BlockSpec(memory_space=space)


def params(mib):
    return pltpu.CompilerParams(vmem_limit_bytes=mib * 1024 * 1024)


def in_hbm():
    return pl.BlockSpec(memory_space=pltpu.HBM)


def dma(count):
    return pltpu.SemaphoreType.DMA((count,))


def cost(flops, moved):
    return pl.CostEstimate(flops=flops, bytes_accessed=moved, transcendentals=0)


def per_species(ref):
    species = ref.shape[0]
    row = lax.broadcasted_iota(jnp.int32, (species, LANES), 0)
    out = jnp.zeros((species, LANES), F32)
    for k in range(species):
        out = jnp.where(row == k, ref[k], out)
    return out


def pack_kernel(prob_ref, offset_hbm, counts_hbm, out_hbm, offset, counts, out, in_sem, out_sem):
    species, owners, slots = offset.shape
    pieces = in_sem.shape[0] // 2
    size = owners // pieces
    loads = []
    for p in range(pieces):
        part = pl.ds(p * size, size)
        for i, (src, dst) in enumerate(((offset_hbm, offset), (counts_hbm, counts))):
            copy = pltpu.make_async_copy(src.at[:, part], dst.at[:, part], in_sem.at[2 * p + i])
            copy.start()
            loads.append(copy)
    prob = per_species(prob_ref)
    square = (1.0 - prob) * (1.0 - prob)
    q = (1.0 / (square * square))[None]
    group = 8
    stores = []
    for p in range(pieces):
        loads[2 * p].wait()
        loads[2 * p + 1].wait()

        def turn(i, carry):
            rows = pl.ds(pl.multiple_of(p * size + i * group, group), group)
            for t in range(slots // LANES):
                lanes = pl.ds(t * LANES, LANES)
                offsets = jnp.swapaxes(offset[:, rows, lanes], 0, 1)
                found = jnp.swapaxes(counts[:, rows, lanes], 0, 1)
                out[rows, :species, lanes] = offsets
                out[rows, species:, lanes] = jnp.where(found > 0, jnp.zeros_like(offsets), q)
            return carry

        lax.fori_loop(0, size // group, turn, 0)
        part = pl.ds(p * size, size)
        copy = pltpu.make_async_copy(out.at[part], out_hbm.at[part], out_sem.at[p])
        copy.start()
        stores.append(copy)
    for copy in stores:
        copy.wait()


def pack_sites(site_offset, site_counts, detect_prob):
    species, owners, slots = site_offset.shape
    pieces = 8
    return pl.pallas_call(
        pack_kernel,
        in_specs=[whole(SMEM), in_hbm(), in_hbm()],
        out_specs=in_hbm(),
        out_shape=jax.ShapeDtypeStruct((owners, 2 * species, slots), F32),
        scratch_shapes=[
            VMEM(site_offset.shape, F32),
            VMEM(site_offset.shape, jnp.int32),
            VMEM((owners, 2 * species, slots), F32),
            dma(2 * pieces),
            dma(pieces),
        ],
        compiler_params=params(56),
        name="pack_sites",
    )(detect_prob, site_offset, site_counts)


def load_row(ref, row):
    return [ref[row, :, t * LANES:(t + 1) * LANES] for t in range(ref.shape[2] // LANES)]


def store_row(ref, row, tiles):
    for t, tile in enumerate(tiles):
        ref[row, :, t * LANES:(t + 1) * LANES] = tile


def factor_row(ref, row, ksq4, lane, count=None):
    center = load_row(ref, row)
    above = load_row(ref, row - 1)
    below = load_row(ref, row + 1)
    total = len(center)
    right = [pltpu.roll(tile, 1, 1) for tile in center]
    left = [pltpu.roll(tile, LANES - 1, 1) for tile in center]
    out = []
    for t in range(count or total):
        from_left = jnp.where(lane == 0, right[t - 1], right[t])
        from_right = jnp.where(lane == LANES - 1, left[(t + 1) % total], left[t])
        out.append(ksq4 * center[t] - ((above[t] + below[t]) + (from_left + from_right)))
    return out


def each_row(first, last, body, chunk=32):
    turns = (last - first) // chunk

    def turn(i, carry):
        for u in range(chunk):
            body(first + i * chunk + u)
        return carry

    lax.fori_loop(0, turns, turn, 0)
    for row in range(first + turns * chunk, last):
        body(row)


class Edges:
    def __init__(self, lane):
        gr, gc = lax.axis_index("gr"), lax.axis_index("gc")
        self.up, self.down, left, right = (
            jnp.where(there, jnp.float32(1.0), jnp.float32(0.0))
            for there in (
                gr > 0,
                gr < lax.axis_size("gr") - 1,
                gc > 0,
                gc < lax.axis_size("gc") - 1,
            )
        )
        self.halo = jnp.where(lane < LANES // 2, right, left)

    def pass_rows(self, first, last, low, high, row_tiles, dst_ref):
        def put(row, scale):
            tiles = row_tiles(row)
            tiles[-1] = tiles[-1] * self.halo
            if scale is not None:
                tiles = [tile * scale for tile in tiles]
            store_row(dst_ref, row, tiles)

        for row in range(first, low):
            put(row, self.up)
        each_row(low, high, lambda row: put(row, None))
        for row in range(high, last):
            put(row, self.down)


def strip_pack(field_ref, width, side):
    rows, species, cols = field_ref.shape
    per_tile = LANES // width
    lane = lax.broadcasted_iota(jnp.int32, (species, LANES), 1) // width
    tiles = []
    for tile in range(rows // per_tile):
        packed = jnp.zeros((species, LANES), F32)
        for p in range(per_tile):
            row = tile * per_tile + p
            if side == 0:
                part = field_ref[row, :, :LANES]
                shift = (p * width) % LANES
            else:
                part = field_ref[row, :, cols - LANES:]
                shift = (p * width + width) % LANES
            if shift:
                part = pltpu.roll(part, shift, 1)
            packed = jnp.where(lane == p, part, packed)
        tiles.append(packed)
    return tiles


def halo_tile(right_tiles, left_tiles, row, width, lane):
    per_tile = LANES // width
    tile, p = row // per_tile, row % per_tile
    shift = (LANES - p * width) % LANES
    from_right = pltpu.roll(right_tiles[tile], shift, 1) if shift else right_tiles[tile]
    shift = (LANES - p * width - width) % LANES
    from_left = pltpu.roll(left_tiles[tile], shift, 1) if shift else left_tiles[tile]
    return jnp.where(lane < width, from_right, jnp.where(lane >= LANES - width, from_left, 0.0))


WIDTHS = (8, 4, 2)
DEPTHS = (6, 4, 2)
TURN = 48
STAGES = 4
LIST = 8


def strip_counts(rows):
    return [rows * width // LANES for width in WIDTHS]


def gather_kernel(first_ref, cells_ref, lat_ref, values_ref, cells_out, list_ref):
    sources, blocks = cells_ref.shape[:2]
    rows, species, cols = lat_ref.shape
    tiles = cols // LANES
    total = sources * blocks
    per_stage = sources // STAGES

    def step(source, spot):
        for j in range(blocks):
            cell = cells_ref[source, j:j + 1, :]
            first = first_ref[source * blocks + j]
            row = jnp.maximum(first, 0) // cols
            live = first >= 0
            at = jnp.where(live, spot, total + TURN)
            wide = jnp.broadcast_to(cell, (species, SB))
            low = wide & (LANES - 1)
            high = (wide // LANES) & (tiles - 1)
            value = jnp.zeros((species, SB), F32)
            for t in range(tiles):
                part = lat_ref[row, :, t * LANES:(t + 1) * LANES]
                picked = jnp.take_along_axis(part, low, axis=1)
                value = jnp.where(high == t, picked, value)
            values_ref[at] = value
            cells_out[at] = wide
            list_ref[LIST + at] = (source * blocks + j) * rows + row
            spot = spot + live.astype(jnp.int32)
        return spot

    count = jnp.int32(0)
    for stage in range(STAGES):
        list_ref[stage] = count
        count = lax.fori_loop(stage * per_stage, (stage + 1) * per_stage, step, count)
    list_ref[STAGES] = count
    for u in range(TURN):
        values_ref[count + u] = jnp.zeros((species, SB), F32)
        cells_out[count + u] = jnp.full((species, SB), -1, jnp.int32)
        list_ref[LIST + count + u] = 0
    room = cells_out.shape[0]
    depth = DEPTHS[0]
    edges = strip_pack(lat_ref, WIDTHS[0], 0) + strip_pack(lat_ref, WIDTHS[0], 1)
    for row in list(range(depth)) + list(range(rows - depth, rows)):
        edges += load_row(lat_ref, row)
    for i, tile in enumerate(edges):
        values_ref[room + i] = tile


def gather_latent(first, site_cells, lat_rows):
    sources, blocks, lanes = site_cells.shape
    rows, species, cols = lat_rows.shape
    room = sources * blocks + 2 * TURN
    strips = strip_counts(rows)[0]
    f32 = lambda *s: jax.ShapeDtypeStruct(s, F32)
    i32 = lambda *s: jax.ShapeDtypeStruct(s, jnp.int32)
    return pl.pallas_call(
        gather_kernel,
        in_specs=[whole(SMEM), whole(), whole()],
        out_specs=[whole()] * 2 + [whole(SMEM)],
        out_shape=[
            f32(room + 2 * strips + 2 * DEPTHS[0] * (cols // LANES), species, lanes),
            i32(room, species, lanes),
            i32(LIST + room),
        ],
        compiler_params=params(56),
        cost_estimate=cost(16 * room * lanes * species, 8 * room * lanes * species),
        name="gather_latent",
    )(first, site_cells, lat_rows)


def hi_lo(value):
    high = value.astype(BF16)
    low = (value - high.astype(F32)).astype(BF16)
    return high, low


def site_kernel(list_hbm, cells_hbm, values_hbm, sites_hbm,
                g_ref, w_ref, left_ref, right_ref, up_ref, down_ref,
                list_ref, cells_ref, values_ref, sites_ref, lat_ref, in_sem, small_sem):
    rows, species, cols = g_ref.shape
    sources, _, slots = sites_ref.shape
    blocks = slots // SB
    tiles = cols // LANES
    list_copy = pltpu.make_async_copy(list_hbm, list_ref, small_sem.at[0])
    list_copy.start()
    loads = []
    for stage in range(STAGES):
        size = sources // STAGES
        last = stage == STAGES - 1
        spots = pl.ds(stage * size * blocks, size * blocks + (TURN if last else 0))
        for i, (src, dst, part) in enumerate((
            (sites_hbm, sites_ref, pl.ds(stage * size, size)),
            (values_hbm, values_ref, spots),
            (cells_hbm, cells_ref, spots),
        )):
            copy = pltpu.make_async_copy(src.at[part], dst.at[part], in_sem.at[3 * stage + i])
            copy.start()
            loads.append(copy)
    tail = pl.ds(cells_ref.shape[0], lat_ref.shape[0])
    lat_copy = pltpu.make_async_copy(values_hbm.at[tail], lat_ref, small_sem.at[1])
    lat_copy.start()
    g_ref[...] = jnp.zeros_like(g_ref)
    w_ref[...] = jnp.zeros_like(w_ref)
    lane_of = lax.broadcasted_iota(jnp.int32, (LANES, SB), 0).astype(jnp.int16)
    one = jnp.ones((LANES, SB), BF16)
    zero = jnp.zeros((LANES, SB), BF16)
    zero16 = jnp.zeros((2 * species, SB), BF16)

    def place(at):
        block = list_ref[LIST + at] // rows
        source = block // blocks
        spot = pl.ds(pl.multiple_of((block % blocks) * SB, SB), SB)
        cell = jnp.concatenate([cells_ref[at]] * 2, axis=0)
        low = (cell & (LANES - 1)).astype(jnp.int16)
        high = jnp.where(cell < 0, -1, (cell // LANES) & (tiles - 1)).astype(jnp.int16)
        eta = values_ref[at] + sites_ref[source, :species, spot]
        ratio = sites_ref[source, species:, spot]
        e = jnp.exp(-eta)
        psi = 1.0 / (1.0 + e)
        ep = e * psi
        weight = ep * psi
        gradient = ep * (1.0 - ratio) / (1.0 + e * ratio)
        both_hi, both_lo = hi_lo(jnp.concatenate([weight, gradient], axis=0))
        hot = jnp.where(lane_of == jnp.concatenate([low] * (LANES // low.shape[0]), axis=0), one, zero)
        placed_hi = []
        placed_lo = []
        for t in range(tiles):
            here = high == t
            placed_hi.append(jnp.where(here, both_hi, zero16))
            placed_lo.append(jnp.where(here, both_lo, zero16))
        left = jnp.concatenate(
            [jnp.concatenate(placed_hi, axis=0), jnp.concatenate(placed_lo, axis=0)], axis=1
        )
        right = jnp.concatenate([hot, hot], axis=1)
        return lax.dot_general(left, right, (((1,), (1,)), ((), ())), preferred_element_type=F32)

    def turn(i, carry):
        at = [i * TURN + u for u in range(TURN)]
        for spot in at:
            placed = place(spot)
            row = list_ref[LIST + spot] % rows
            for t in range(tiles):
                lanes = pl.ds(t * LANES, LANES)
                start = 2 * species * t
                w_ref[row, :, lanes] += placed[start:start + species]
                g_ref[row, :, lanes] += placed[start + species:start + 2 * species]
        return carry

    list_copy.wait()
    for stage in range(STAGES):
        for copy in loads[3 * stage:3 * stage + 3]:
            copy.wait()
        first = list_ref[stage] // TURN
        end = list_ref[stage + 1]
        if stage == STAGES - 1:
            end = end + TURN - 1
        lax.fori_loop(first, end // TURN, turn, 0)

    lat_copy.wait()
    lat_strips = strip_counts(rows)[0]
    for side, ref in ((0, left_ref), (1, right_ref)):
        strips = [lat_ref[side * lat_strips + i] for i in range(lat_strips)]
        strips += strip_pack(g_ref, WIDTHS[1], side) + strip_pack(w_ref, WIDTHS[2], side)
        for i, strip in enumerate(strips):
            ref[i] = strip
    for ref, low_side in ((up_ref, True), (down_ref, False)):
        i = DEPTHS[0] * tiles
        base = 2 * lat_strips + (0 if low_side else i)
        for t in range(i):
            ref[t] = lat_ref[base + t]
        for field, depth in zip((g_ref, w_ref), DEPTHS[1:]):
            for row in range(depth) if low_side else range(rows - depth, rows):
                for tile in load_row(field, row):
                    ref[i] = tile
                    i += 1
        for j in range(i, ref.shape[0]):
            ref[j] = jnp.zeros((species, LANES), F32)


def site_terms(values, cells, block_list, sites, rows, cols):
    species = values.shape[1]
    counts = strip_counts(rows)
    strips = sum(counts)
    edge_tiles = sum(DEPTHS) * (cols // LANES) + 2 * sum(counts)
    shape = lambda *s: jax.ShapeDtypeStruct(s, F32)
    return pl.pallas_call(
        site_kernel,
        in_specs=[in_hbm()] * 4,
        out_specs=[whole()] * 6,
        out_shape=[
            shape(rows, species, cols),
            shape(rows, species, cols),
            shape(strips, species, LANES),
            shape(strips, species, LANES),
            shape(edge_tiles, species, LANES),
            shape(edge_tiles, species, LANES),
        ],
        scratch_shapes=[
            SMEM(block_list.shape, jnp.int32),
            VMEM(cells.shape, jnp.int32),
            VMEM(cells.shape, F32),
            VMEM(sites.shape, F32),
            VMEM((values.shape[0] - cells.shape[0], species, LANES), F32),
            dma(3 * STAGES),
            dma(2),
        ],
        compiler_params=params(48),
        name="site_terms",
    )(block_list, cells, values, sites)


RIM = 6
PADS = (6, 4, 2)
MID_PAD = 5


class Krylov:
    def __init__(self, ksq_ref, scratch):
        self.lx, self.bx, self.wx, self.mid = scratch
        species = ksq_ref.shape[0]
        self.lane = lax.broadcasted_iota(jnp.int32, (species, LANES), 1)
        ksq = per_species(ksq_ref)
        self.ksq4 = ksq + 4.0
        self.scale = 4.0 * math.pi * ksq
        self.edges = Edges(self.lane)
        self.zero = jnp.zeros((species, LANES), F32)

    def factor(self, src, pad, row, count=None):
        return factor_row(src, row + pad, self.ksq4, self.lane, count)

    def passes(self, first, last, low, high):
        lx, bx, wx, mid = self.lx, self.bx, self.wx, self.mid
        scale = self.scale

        def run(reach, pad, row_tiles, dst):
            f, l = first - reach, last + reach
            self.edges.pass_rows(
                f + pad, l + pad, max(f, low) + pad, min(l, high) + pad, lambda r: row_tiles(r - pad), dst
            )

        def right_side(r):
            return [g - scale * f for g, f in zip(load_row(bx, r + 4), self.factor(mid, MID_PAD, r))]

        def image(r):
            both = zip(self.factor(mid, MID_PAD, r), load_row(wx, r + 2), load_row(bx, r + 4))
            return [scale * f + w * b for f, w, b in both]

        run(5, MID_PAD, lambda r: self.factor(lx, 6, r), mid)
        run(4, 4, right_side, bx)
        run(3, MID_PAD, lambda r: self.factor(bx, 4, r), mid)
        run(2, 6, image, lx)
        run(1, MID_PAD, lambda r: self.factor(lx, 6, r), mid)

    def last(self, row, tiles, outs, to, sums):
        bb, bh, hh, hh2 = sums
        for t, f in enumerate(self.factor(self.mid, MID_PAD, row, tiles)):
            lanes = pl.ds(t * LANES, LANES)
            b = self.bx[row + 4, :, lanes]
            h = self.lx[row + 6, :, lanes]
            h2 = self.scale * f + self.wx[row + 2, :, lanes] * h
            for ref, value in zip(outs, (b, h, h2)):
                ref[to, :, lanes] = value
            bb = bb + b * b
            bh = bh + b * h
            hh = hh + h * h
            hh2 = hh2 + h * h2
        return bb, bh, hh, hh2


def strips_of(ref, base, rows):
    out = []
    for count in strip_counts(rows):
        out.append([ref[base + i] for i in range(count)])
        base += count
    return out


def inner_kernel(ksq_ref, lat_ref, g_ref, w_ref, right_ref, left_ref, b_out, h_out, h2_out, sums_ref, *scratch):
    rows, species, cols = g_ref.shape
    krylov = Krylov(ksq_ref, scratch)
    right = strips_of(right_ref, 0, rows)
    left = strips_of(left_ref, 0, rows)
    halo = pl.ds(cols, LANES)
    for field, ext, pad, width, r, l in zip((lat_ref, g_ref, w_ref), scratch, PADS, WIDTHS, right, left):
        ext[pad:rows + pad, :, :cols] = field[...]
        for row in range(rows):
            ext[pad + row, :, halo] = halo_tile(r, l, row, width, krylov.lane)
    krylov.passes(RIM, rows - RIM, 0, rows)
    wanted = rows - 2 * RIM
    group = max(d for d in range(1, 17) if wanted % d == 0)

    def turn(i, sums):
        for u in range(group):
            row = RIM + i * group + u
            sums = krylov.last(row, cols // LANES, (b_out, h_out, h2_out), row, sums)
        return sums

    sums = lax.fori_loop(0, wanted // group, turn, (krylov.zero,) * 4)
    for i, total in enumerate(sums):
        sums_ref[i] = total


def scratch_of(rows, species, cols):
    return [VMEM((rows + 2 * pad, species, cols + LANES), F32) for pad in PADS + (MID_PAD,)]


def inner(ksq, lat_rows, g, w, right, left):
    rows, species, cols = g.shape
    shape = lambda *s: jax.ShapeDtypeStruct(s, F32)
    field = shape(rows, species, cols)
    return pl.pallas_call(
        inner_kernel,
        in_specs=[whole(SMEM)] + [whole()] * 5,
        out_specs=[whole()] * 4,
        out_shape=[field, field, field, shape(4, species, LANES)],
        scratch_shapes=scratch_of(rows, species, cols),
        compiler_params=params(20),
        cost_estimate=cost(80 * rows * species * cols, 64 * rows * species * cols),
        name="krylov_inner",
    )(ksq, lat_rows, g, w, right, left)


def rim_kernel(ksq_ref, lat_ref, g_ref, w_ref, right_ref, left_ref, up_ref, down_ref, sums_ref,
               b_out, h_out, h2_out, part_ref, *scratch):
    rows, species, cols = g_ref.shape
    tiles = cols // LANES
    krylov = Krylov(ksq_ref, scratch)
    lane = krylov.lane
    fields = (lat_ref, g_ref, w_ref)
    halo = pl.ds(cols, LANES)
    own_right = strips_of(right_ref, 0, rows)
    own_left = strips_of(left_ref, 0, rows)
    base = sum(DEPTHS) * tiles
    sums = tuple(sums_ref[i] for i in range(4))
    for ref, above in ((up_ref, True), (down_ref, False)):
        start = 0 if above else rows - RIM
        came_right = strips_of(ref, base, rows)
        came_left = strips_of(ref, base + sum(strip_counts(rows)), rows)
        i = 0
        for n, (field, ext, pad, width) in enumerate(zip(fields, scratch, PADS, WIDTHS)):
            for local in range(-pad, RIM + pad):
                own = start + local
                to = local + pad
                if 0 <= own < rows:
                    store_row(ext, to, load_row(field, own))
                    ext[to, :, halo] = halo_tile(own_right[n], own_left[n], own, width, lane)
                else:
                    for t in range(tiles):
                        ext[to, :, t * LANES:(t + 1) * LANES] = ref[i]
                        i += 1
                    came = own % rows
                    ext[to, :, halo] = halo_tile(came_right[n], came_left[n], came, width, lane)
        if above:
            krylov.passes(0, RIM, 0, RIM + 6)
        else:
            krylov.passes(0, RIM, -6, RIM)
        for row in range(RIM):
            to = row if above else RIM + row
            sums = krylov.last(row, tiles, (b_out, h_out, h2_out), to, sums)
    lane_row = lax.broadcasted_iota(jnp.int32, part_ref.shape, 1)
    part = jnp.zeros(part_ref.shape, F32)
    for i, total in enumerate(sums):
        narrow = jnp.sum(total, axis=0, keepdims=True)
        narrow = jnp.sum(narrow, axis=1, keepdims=True)
        part = jnp.where(lane_row == i, narrow, part)
    part_ref[...] = part


def rim(ksq, lat_rows, g, w, right, left, from_up, from_down, sums, devices):
    rows, species, cols = g.shape
    shape = lambda *s: jax.ShapeDtypeStruct(s, F32)
    field = shape(2 * RIM, species, cols)
    return pl.pallas_call(
        rim_kernel,
        in_specs=[whole(SMEM)] + [whole()] * 8,
        out_specs=[whole()] * 4,
        out_shape=[field, field, field, shape(devices, LANES)],
        scratch_shapes=scratch_of(RIM, species, cols),
        compiler_params=params(16),
        name="krylov_rim",
    )(ksq, lat_rows, g, w, right, left, from_up, from_down, sums)


def finish_kernel(parts_ref, b_ref, h_ref, h2_ref, b_rim, h_rim, h2_rim, step_ref, residual_ref):
    total = jnp.sum(parts_ref[...], axis=0, keepdims=True)
    lane = lax.broadcasted_iota(jnp.int32, total.shape, 1)

    def pick(i):
        return jnp.sum(jnp.where(lane == i, total, 0.0), axis=1, keepdims=True)

    bb, bh, hh, hh2 = (pick(i) for i in range(4))
    alpha = bb / bh
    rr = bb - 2.0 * alpha * bh + alpha * alpha * hh
    beta = rr / bb
    grown = 1.0 + beta
    curve = grown * grown * bh - 2.0 * grown * alpha * hh + alpha * alpha * hh2
    later = rr / curve
    c0 = (alpha + later * grown)[None]
    c1 = (later * alpha)[None]

    def put(first, b, h, h2):
        spot = pl.ds(first, b.shape[0])
        step_ref[:, spot, :] = jnp.swapaxes(c0 * b - c1 * h, 0, 1)
        residual_ref[:, spot, :] = jnp.swapaxes(b - c0 * h + c1 * h2, 0, 1)

    group = b_ref.shape[0]
    put(0, b_ref[...], h_ref[...], h2_ref[...])
    refs = ((b_ref, b_rim), (h_ref, h_rim), (h2_ref, h2_rim))

    @pl.when(pl.program_id(0) == 0)
    def _():
        put(0, *(jnp.concatenate([edge[:RIM], ref[RIM:8]], axis=0) for ref, edge in refs))

    @pl.when(pl.program_id(0) == pl.num_programs(0) - 1)
    def _():
        put(group - 8, *(jnp.concatenate([ref[group - 8:group - RIM], edge[RIM:]], axis=0) for ref, edge in refs))


def finish(parts, fields, rims):
    rows, species, cols = fields[0].shape
    group = rows // 2
    field = pl.BlockSpec((group, species, cols), lambda i: (i, 0, 0))
    edge = pl.BlockSpec((2 * RIM, species, cols), lambda i: (0, 0, 0))
    out = pl.BlockSpec((species, group, cols), lambda i: (0, i, 0))
    shape = jax.ShapeDtypeStruct((species, rows, cols), F32)
    return pl.pallas_call(
        finish_kernel,
        grid=(rows // group,),
        in_specs=[pl.BlockSpec(parts.shape, lambda i: (0, 0))] + [field] * 3 + [edge] * 3,
        out_specs=[out, out],
        out_shape=[shape, shape],
        compiler_params=params(28),
        name="finish",
    )(parts, *fields, *rims)


def neighbour_pairs(count):
    forward = [(i, i + 1) for i in range(count - 1)]
    backward = [(target, source) for source, target in forward]
    return forward, backward


def per_device(latent, site_offset, site_counts, site_cells, detect_prob, kappa_sq):
    species, rows, cols = latent.shape
    n_gr, n_gc = lax.axis_size("gr"), lax.axis_size("gc")
    down_pairs, up_pairs = neighbour_pairs(n_gr)
    right_pairs, left_pairs = neighbour_pairs(n_gc)
    sites = lax.all_to_all(
        pack_sites(site_offset, site_counts, detect_prob), MESH, split_axis=0, concat_axis=0, tiled=True
    )
    lat_rows = jnp.transpose(latent, (1, 0, 2))
    first = site_cells[:, ::SB].reshape(-1)
    site_cells = site_cells.reshape(site_cells.shape[0], -1, SB)
    blocks = gather_latent(first, site_cells, lat_rows)

    g, w, to_left, to_right, to_up, to_down = site_terms(*blocks, sites, rows, cols)
    from_left = lax.ppermute(to_right, "gc", right_pairs)
    from_right = lax.ppermute(to_left, "gc", left_pairs)
    strips = jnp.concatenate([from_right, from_left], axis=0)
    spot = (to_up.shape[0] - strips.shape[0], 0, 0)
    to_up = lax.dynamic_update_slice(to_up, strips, spot)
    to_down = lax.dynamic_update_slice(to_down, strips, spot)
    from_up = lax.ppermute(to_down, "gr", down_pairs)
    from_down = lax.ppermute(to_up, "gr", up_pairs)

    near = (kappa_sq, lat_rows, g, w, from_right, from_left)
    *fields, sums = inner(*near)
    *rims, part = rim(*near, from_up, from_down, sums, n_gr * n_gc)
    parts = lax.all_to_all(part, MESH, split_axis=0, concat_axis=0, tiled=True)
    return finish(parts, fields, rims)


def solution(mesh):
    in_specs = (
        P(None, "gr", "gc"),
        P(None, ("gr", "gc"), None),
        P(None, ("gr", "gc"), None),
        P(("gr", "gc"), None),
        P(),
        P(),
    )
    out_specs = (P(None, "gr", "gc"), P(None, "gr", "gc"))
    return jax.shard_map(
        per_device, mesh=mesh, in_specs=in_specs, out_specs=out_specs, check_vma=False
    )
```
